32 devices in a mesh: dp: 8 (over z, x), mp: 4 (over y, core).
Axes of the slice: x: 2, y: 2, z: 4, core: 2. Of those that a mesh axis runs over, the one named last changes fastest.
Arguments:
- block_input: bfloat16 [2048, 1152], P(('dp', 'mp')), may hold values from -6 to 6
- segments: int32 [8, 512], P('dp'), may hold values from 0 to 4, as said below
- attend_gain: bfloat16 [2, 576], replicated, may hold values from 0.5 to 1.5
- query_weight: bfloat16 [2, 576, 576], P(None, 'dp', 'mp'), may hold values from -0.25 to 0.25
- key_weight: bfloat16 [2, 576, 192], P(None, 'dp', 'mp'), may hold values from -0.25 to 0.25
- value_weight: bfloat16 [2, 576, 192], P(None, 'dp', 'mp'), may hold values from -0.25 to 0.25
- mix_weight: bfloat16 [2, 576, 576], P(None, 'mp', 'dp'), may hold values from -1 to 1
- feed_gain: bfloat16 [2, 576], replicated, may hold values from 0.5 to 1.5
- gate_weight: bfloat16 [2, 576, 1536], P(None, 'dp', 'mp'), may hold values from -0.25 to 0.25
- up_weight: bfloat16 [2, 576, 1536], P(None, 'dp', 'mp'), may hold values from -0.25 to 0.25
- down_weight: bfloat16 [2, 1536, 576], P(None, 'mp', 'dp'), may hold values from -0.3125 to 0.3125
- cotangent: bfloat16 [2048, 1152], P(('dp', 'mp')), may hold values from -6 to 6
Outputs:
- block_output: bfloat16 [2048, 1152], P(('dp', 'mp'))
- input_grad: float32 [2048, 1152], P(('dp', 'mp'))
- attend_gain_grad: float32 [2, 576], replicated
- query_grad: float32 [2, 576, 576], P(None, 'dp', 'mp')
- key_grad: float32 [2, 576, 192], P(None, 'dp', 'mp')
- value_grad: float32 [2, 576, 192], P(None, 'dp', 'mp')
- mix_grad: float32 [2, 576, 576], P(None, 'mp', 'dp')
- feed_gain_grad: float32 [2, 576], replicated
- gate_grad: float32 [2, 576, 1536], P(None, 'dp', 'mp')
- up_grad: float32 [2, 576, 1536], P(None, 'dp', 'mp')
- down_grad: float32 [2, 1536, 576], P(None, 'mp', 'dp')
The draws below stay inside these ranges and needn't reach their ends.
Inputs may be any that keep to these rules, and one draw needn't show every extreme that they name: `segments`: segment numbers never fall along a sequence and may skip values; in every sequence one segment holds both position 127 and position 384.
All inputs are finite; a program needn't handle non-finite values.
Results may differ from the reference program's by a relative error of at most 0.034.
Values may be sent and summed in bfloat16 or wider, within the bound.
A program may use at most 128 MiB of HBM per device.

```python
import math
import jax
import jax.numpy as jnp
from jax import lax

HEADS = 9
KV_HEADS = 3
HEAD_DIM = 64
FF = 1536
D = 576
KVW = 192
LAYERS = 2
TOK_DEV = 512
SEQS = 8
TOKENS = 4096


def draw_segments(key, part):
    key = jax.random.fold_in(key, 7)
    low_key, high_key = jax.random.split(key)
    low_cuts = jax.random.randint(low_key, (SEQS, 2), 0, TOK_DEV // 4)
    high_cuts = jax.random.randint(high_key, (SEQS, 2), 3 * TOK_DEV // 4 + 1, TOK_DEV + 1)
    cut_points = jnp.concatenate([low_cuts, high_cuts], axis=1).astype(jnp.int32)
    token_index = jnp.arange(TOK_DEV, dtype=jnp.int32)
    passed = (cut_points[:, None, :] <= token_index[None, :, None]) & (cut_points[:, None, :] > 0)
    return jnp.sum(passed.astype(jnp.int32), axis=2).astype(jnp.int32)


def level_of(key, shape, pieces, low, largest):
    def one(position, parts):
        steps = jax.random.uniform(jax.random.fold_in(jax.random.fold_in(key, 6), position), (parts,), jnp.float32, low / len(pieces), largest / len(pieces))
        return jnp.repeat(jnp.exp(steps), shape[position] // parts).reshape((-1,) + (1,) * (len(shape) - position - 1))

    level = one(*pieces[0])
    for cut in pieces[1:]:
        level = level * one(*cut)
    return level


def noise(key, dims, width, bound, cuts=(), kind=jnp.bfloat16):
    drawn = width * jax.random.normal(key, dims, jnp.float32)
    if cuts:
        drawn = drawn * level_of(key, dims, cuts, -0.22, 0.18)
    return jnp.clip(drawn, -bound, bound).astype(kind)


def setup_inputs(seed: int = 0) -> dict:
    splits = jax.random.split(jax.random.key(seed), 13)
    block_input = noise(splits[0], (TOKENS // 2, 2 * D), 1.0, 6.0, ((0, 32),))
    segments = draw_segments(jax.random.fold_in(splits[12], 71), 0)
    attend_gain = jnp.clip(1.0 + 0.1 * jax.random.normal(splits[2], (LAYERS, D), jnp.float32), 0.5, 1.5).astype(jnp.bfloat16)
    query_weight = noise(splits[3], (LAYERS, D, D), D ** -0.5, 0.25, ((1, 8), (2, 4)))
    key_weight = noise(splits[4], (LAYERS, D, KVW), D ** -0.5, 0.25, ((1, 8), (2, 4)))
    value_weight = noise(splits[5], (LAYERS, D, KVW), D ** -0.5, 0.25, ((1, 8), (2, 4)))
    mix_weight = noise(splits[6], (LAYERS, D, D), (D // 16) ** -0.5, 1.0, ((1, 4), (2, 8)))
    feed_gain = jnp.clip(1.0 + 0.1 * jax.random.normal(splits[7], (LAYERS, D), jnp.float32), 0.5, 1.5).astype(jnp.bfloat16)
    gate_weight = noise(splits[8], (LAYERS, D, FF), D ** -0.5, 0.25, ((1, 8), (2, 4)))
    up_weight = noise(splits[9], (LAYERS, D, FF), D ** -0.5, 0.25, ((1, 8), (2, 4)))
    down_weight = noise(splits[10], (LAYERS, FF, D), (FF // 4) ** -0.5, 0.3125, ((1, 4), (2, 8)))
    cotangent = noise(splits[11], (TOKENS // 2, 2 * D), 1.0, 6.0, ((0, 32),))
    return dict(block_input=block_input, segments=segments, attend_gain=attend_gain, query_weight=query_weight, key_weight=key_weight, value_weight=value_weight, mix_weight=mix_weight, feed_gain=feed_gain, gate_weight=gate_weight, up_weight=up_weight, down_weight=down_weight, cotangent=cotangent)


@jax.custom_vjp
def low(v):
    return lax.optimization_barrier(v.astype(jnp.bfloat16)).astype(jnp.float32)

@jax.custom_vjp
def low_back(v):
    return v

def low_keep(v):
    return (low(v), None)

def low_pass(kept, grad):
    return (grad,)

def back_keep(v):
    return (v, None)

def back_low(kept, grad):
    return (low(grad),)
low.defvjp(low_keep, low_pass)
low_back.defvjp(back_keep, back_low)
norm_eps = 1e-05
rope_base = 100000.0
masked_value = -1e+30

def doc_positions(seg_ids):
    length_all = seg_ids.shape[-1]
    token_index = jnp.broadcast_to(jnp.arange(length_all, dtype=jnp.int32), seg_ids.shape)
    starts = jnp.concatenate([token_index[..., :1] == 0, seg_ids[..., 1:] != seg_ids[..., :-1]], axis=-1)
    doc_start = lax.cummax(jnp.where(starts, token_index, 0), axis=seg_ids.ndim - 1)
    return token_index - doc_start

def rope_tables(positions):
    half_dim = HEAD_DIM // 2
    exponents = jnp.arange(half_dim, dtype=jnp.float32) * (2.0 / HEAD_DIM)
    inverse = jnp.exp(-math.log(rope_base) * exponents)
    angles = positions.astype(jnp.float32)[..., None] * inverse
    cosine = jnp.cos(angles)
    sine = jnp.sin(angles)
    return (jnp.concatenate([cosine, cosine], axis=-1), jnp.concatenate([sine, sine], axis=-1))

def rotate(values, cosine, sine):
    half_dim = values.shape[-1] // 2
    turned = jnp.concatenate([-values[..., half_dim:], values[..., :half_dim]], axis=-1)
    return values * cosine[..., None, :] + turned * sine[..., None, :]

def matmul_high(left, right):
    return jnp.dot(left, right, precision=lax.Precision.HIGHEST, preferred_element_type=jnp.float32)

def norm_rows(residual, gain):
    rounded = low(residual)
    row_scale = lax.rsqrt(lax.optimization_barrier(jnp.mean(rounded * rounded, axis=-1, keepdims=True)) + norm_eps)
    return low(rounded * row_scale * gain)

def attend_group(queries, keys_turned, values_used, seg_ids):
    group_size = HEADS // KV_HEADS
    keys_wide = jnp.repeat(keys_turned, group_size, axis=2)
    values_wide = jnp.repeat(values_used, group_size, axis=2)
    scores = low_back(jnp.einsum('gqhd,gkhd->ghqk', queries, keys_wide, precision=lax.Precision.HIGHEST))
    logits = scores * (1.0 / math.sqrt(HEAD_DIM))
    token_index = jnp.arange(seg_ids.shape[1], dtype=jnp.int32)
    allowed = (token_index[None, :, None] >= token_index[None, None, :]) & (seg_ids[:, :, None] == seg_ids[:, None, :])
    logits = jnp.where(allowed[:, None], logits, masked_value)
    row_max = lax.optimization_barrier(jnp.max(logits, axis=-1, keepdims=True))
    raised = jnp.exp(logits - row_max)
    weights = raised / lax.optimization_barrier(jnp.sum(raised, axis=-1, keepdims=True))
    mixed = jnp.einsum('ghqk,gkhd->gqhd', low(weights), values_wide, precision=lax.Precision.HIGHEST)
    return mixed.reshape(mixed.shape[0], mixed.shape[1], -1)

def block_attend(block_items):
    return attend_group(*block_items)

def forward(block_input, attend_gain, query_weight, key_weight, value_weight, mix_weight, feed_gain, gate_weight, up_weight, down_weight, segments):
    cosine, sine = rope_tables(doc_positions(segments))
    per_block = math.gcd(SEQS, max(1, 4096 // TOK_DEV))
    blocks = SEQS // per_block

    def shape_blocks(array):
        return array.reshape((blocks, per_block) + array.shape[1:])
    residual = block_input
    for layer_index in range(LAYERS):
        normed = norm_rows(residual, attend_gain[layer_index])
        queries = low_back(low(matmul_high(normed, query_weight[layer_index])))
        key_rows = low_back(low(matmul_high(normed, key_weight[layer_index])))
        values = low_back(low(matmul_high(normed, value_weight[layer_index])))
        queries = low(rotate(queries.reshape(SEQS, TOK_DEV, HEADS, HEAD_DIM), cosine, sine))
        key_rows = low(rotate(key_rows.reshape(SEQS, TOK_DEV, KV_HEADS, HEAD_DIM), cosine, sine))
        values = values.reshape(SEQS, TOK_DEV, KV_HEADS, HEAD_DIM)
        mixed = lax.map(jax.checkpoint(block_attend), (shape_blocks(queries), shape_blocks(key_rows), shape_blocks(values), shape_blocks(segments)))
        mixed = low_back(low(mixed.reshape(TOKENS, D)))
        residual = residual + low_back(matmul_high(mixed, mix_weight[layer_index]))
        normed = norm_rows(residual, feed_gain[layer_index])
        gate_out = low_back(matmul_high(normed, gate_weight[layer_index]))
        up_out = low_back(matmul_high(normed, up_weight[layer_index]))
        hidden = low(jax.nn.silu(gate_out) * up_out)
        residual = residual + low_back(matmul_high(hidden, down_weight[layer_index]))
    return residual

def reference(block_input, segments, attend_gain, query_weight, key_weight, value_weight, mix_weight, feed_gain, gate_weight, up_weight, down_weight, cotangent):
    stream = block_input.reshape(TOKENS, D)
    floats = tuple((array.astype(jnp.float32) for array in (stream, attend_gain, query_weight, key_weight, value_weight, mix_weight, feed_gain, gate_weight, up_weight, down_weight)))

    def forward_all(*values):
        return forward(*values, segments)
    result, pullback = jax.vjp(forward_all, *floats)
    gradients = pullback(cotangent.reshape(TOKENS, D).astype(jnp.float32))
    return (result.reshape(TOKENS // 2, 2 * D).astype(jnp.bfloat16), gradients[0].reshape(TOKENS // 2, 2 * D), gradients[1], gradients[2], gradients[3], gradients[4], gradients[5], gradients[6], gradients[7], gradients[8], gradients[9])
```

```python
import functools
import math

import jax
import jax.numpy as jnp
from jax import lax
from jax.experimental import pallas as pl
from jax.experimental.pallas import tpu as pltpu
from jax.sharding import PartitionSpec as P

HEADS = 9
KV_HEADS = 3
HEAD_DIM = 64
LAYERS = 2


norm_eps = 1e-05
rope_base = 100000.0
masked_value = -1e30


def push_kernel(axis, peers, n_ag, n_a2a, *refs):
    count = n_ag + n_a2a
    ins, outs = refs[:count], refs[count : 2 * count]
    send_sem, recv_sem, local_sem = refs[2 * count :]
    me = lax.axis_index(axis)
    barrier = pltpu.get_barrier_semaphore()
    for step in range(1, peers):
        pl.semaphore_signal(
            barrier,
            inc=1,
            device_id={axis: lax.rem(me + step, peers)},
            device_id_type=pl.DeviceIdType.MESH,
        )
    pl.semaphore_wait(barrier, peers - 1)
    copies = []
    for step in range(1, peers):
        peer = lax.rem(me + step, peers)
        for i in range(count):
            copy = pltpu.make_async_remote_copy(
                src_ref=ins[i] if i < n_ag else ins[i].at[peer],
                dst_ref=outs[i].at[me],
                send_sem=send_sem.at[i, step],
                recv_sem=recv_sem.at[i, step],
                device_id={axis: peer},
                device_id_type=pl.DeviceIdType.MESH,
            )
            copy.start()
            copies.append(copy)
    for i in range(count):
        local = pltpu.make_async_copy(
            ins[i] if i < n_ag else ins[i].at[me], outs[i].at[me], local_sem.at[i]
        )
        local.start()
        copies.append(local)
    for copy in copies:
        copy.wait()


def exchange(number, axis, whole=(), split=()):
    peers = lax.axis_size(axis)
    count = len(whole) + len(split)
    shapes = [jax.ShapeDtypeStruct((peers, *a.shape), a.dtype) for a in whole]
    shapes += [jax.ShapeDtypeStruct(a.shape, a.dtype) for a in split]
    size = sum(math.prod(s.shape) * s.dtype.itemsize for s in shapes)
    space = pltpu.VMEM if size < 6_000_000 else pl.ANY
    return pl.pallas_call(
        functools.partial(push_kernel, axis, peers, len(whole), len(split)),
        out_shape=shapes,
        in_specs=[pl.BlockSpec(memory_space=space)] * count,
        out_specs=[pl.BlockSpec(memory_space=space)] * count,
        scratch_shapes=[
            pltpu.SemaphoreType.DMA((count, peers)),
            pltpu.SemaphoreType.DMA((count, peers)),
            pltpu.SemaphoreType.DMA((count,)),
        ],
        compiler_params=pltpu.CompilerParams(
            collective_id=number, has_side_effects=True, vmem_limit_bytes=40 * 1024 * 1024
        ),
        name="push_" + axis,
    )(*whole, *split)


def doc_positions(seg_ids):
    length_all = seg_ids.shape[-1]
    token_index = jnp.arange(length_all, dtype=jnp.int32)
    starts = jnp.concatenate(
        [token_index[..., :1] == 0, seg_ids[..., 1:] != seg_ids[..., :-1]], axis=-1
    )
    doc_start = lax.cummax(jnp.where(starts, token_index, 0), axis=seg_ids.ndim - 1)
    return token_index - doc_start


def rope_tables(positions):
    half_dim = HEAD_DIM // 2
    exponents = jnp.arange(half_dim, dtype=jnp.float32) * (2.0 / HEAD_DIM)
    inverse = jnp.exp(-math.log(rope_base) * exponents)
    angles = positions.astype(jnp.float32)[..., None] * inverse
    cosine = jnp.cos(angles)
    sine = jnp.sin(angles)
    return (jnp.concatenate([cosine, cosine], axis=-1), jnp.concatenate([sine, sine], axis=-1))


def rotate(values, cosine, sine):
    half_dim = values.shape[-1] // 2
    turned = jnp.concatenate([-values[..., half_dim:], values[..., :half_dim]], axis=-1)
    return values * cosine[..., None, :] + turned * sine[..., None, :]


def matmul_f32(left, right):
    return jnp.dot(left, right, preferred_element_type=jnp.float32)


def inner_rows(left, right):
    return lax.dot_general(
        left, right, (((0,), (0,)), ((), ())), preferred_element_type=jnp.float32
    )


def inner_cols(left, right):
    return lax.dot_general(
        left, right, (((1,), (1,)), ((), ())), preferred_element_type=jnp.float32
    )


def norm_in(residual, gain):
    rows_f32 = residual.astype(jnp.bfloat16).astype(jnp.float32)
    row_scale = lax.rsqrt(jnp.mean(rows_f32 * rows_f32, axis=1, keepdims=True) + norm_eps)
    normed = (rows_f32 * row_scale * gain.astype(jnp.float32)).astype(jnp.bfloat16)
    return (rows_f32, row_scale, normed)


def summed(pieces):
    return jnp.sum(pieces.astype(jnp.float32), axis=0)


def columns_over(gathered):
    peers, rows, width = gathered.shape
    return jnp.moveaxis(gathered, 0, 1).reshape(rows, peers * width)


def norm_back(grad_normed, rows_f32, row_scale, gain):
    width = rows_f32.shape[1]
    gain_f32 = gain.astype(jnp.float32)
    cubed = row_scale * row_scale * row_scale
    inner = jnp.sum(grad_normed * gain_f32 * rows_f32, axis=1, keepdims=True)
    resid_grad = gain_f32 * row_scale * grad_normed - rows_f32 * cubed * inner / width
    gain_term = jnp.sum(grad_normed * rows_f32 * row_scale, axis=0)
    return (resid_grad, gain_term)


def head_views(query_turned, keys_all, values_all):
    own_rows = query_turned.shape[0]
    group_size = HEADS // KV_HEADS
    query_heads = query_turned.reshape(own_rows, KV_HEADS, group_size, HEAD_DIM)
    key_heads = keys_all.reshape(keys_all.shape[0], KV_HEADS, HEAD_DIM)
    value_heads = values_all.reshape(values_all.shape[0], KV_HEADS, HEAD_DIM)
    return (query_heads, key_heads, value_heads)


def masked_logits(query_heads, key_heads, allowed):
    scores = jnp.einsum(
        "qkgd,tkd->kgqt", query_heads, key_heads, preferred_element_type=jnp.float32
    )
    return jnp.where(allowed, scores * (1.0 / math.sqrt(HEAD_DIM)), masked_value)


def attend(query_turned, keys_all, values_all, allowed):
    query_heads, key_heads, value_heads = head_views(query_turned, keys_all, values_all)
    logits = masked_logits(query_heads, key_heads, allowed)
    row_max = jnp.max(logits, axis=3, keepdims=True)
    raised = jnp.exp(logits - row_max)
    row_total = jnp.sum(raised, axis=3, keepdims=True)
    weights_low = (raised / row_total).astype(jnp.bfloat16)
    mixed = jnp.einsum(
        "kgqt,tkd->qkgd", weights_low, value_heads, preferred_element_type=jnp.float32
    )
    return (mixed.reshape(query_turned.shape[0], -1), row_max + jnp.log(row_total))


def attend_back(query_turned, keys_all, values_all, allowed, log_total, grad_mixed):
    query_heads, key_heads, value_heads = head_views(query_turned, keys_all, values_all)
    logits = masked_logits(query_heads, key_heads, allowed)
    weights = jnp.exp(logits - log_total)
    grad_heads = grad_mixed.reshape(query_heads.shape)
    grad_weights = jnp.einsum(
        "qkgd,tkd->kgqt", grad_heads, value_heads, preferred_element_type=jnp.float32
    )
    delta = jnp.sum(weights * grad_weights, axis=3, keepdims=True)
    grad_scores = (weights * (grad_weights - delta) * (1.0 / math.sqrt(HEAD_DIM))).astype(
        jnp.bfloat16
    )
    grad_query = jnp.einsum(
        "kgqt,tkd->qkgd", grad_scores, key_heads, preferred_element_type=jnp.float32
    )
    grad_keys = jnp.einsum(
        "kgqt,qkgd->tkd", grad_scores, query_heads, preferred_element_type=jnp.float32
    )
    grad_values = jnp.einsum(
        "kgqt,qkgd->tkd",
        weights.astype(jnp.bfloat16),
        grad_heads,
        preferred_element_type=jnp.float32,
    )
    row_count = keys_all.shape[0]
    return (
        grad_query.reshape(query_turned.shape[0], -1),
        grad_keys.reshape(row_count, -1),
        grad_values.reshape(row_count, -1),
    )


def on_device(
    block_input,
    segments,
    attend_gain,
    query_weight,
    key_weight,
    value_weight,
    mix_weight,
    feed_gain,
    gate_weight,
    up_weight,
    down_weight,
    cotangent,
):
    bf16, f32 = jnp.bfloat16, jnp.float32
    width = block_input.shape[1] // 2
    own_rows = block_input.shape[0] * 2
    mp = lax.axis_size("mp")
    dp = lax.axis_size("dp")
    row_count = own_rows * mp
    first_row = lax.axis_index("mp") * own_rows
    qw, kw, ff = query_weight.shape[2], key_weight.shape[2], gate_weight.shape[2]
    depth = query_weight.shape[1]
    aw = 2 * qw + 2 * kw
    packed = jnp.concatenate(
        [
            query_weight,
            key_weight,
            value_weight,
            jnp.swapaxes(mix_weight, 1, 2),
            gate_weight,
            up_weight,
            jnp.swapaxes(down_weight, 1, 2),
        ],
        axis=2,
    )
    total_width = packed.shape[2]
    packed = packed.reshape(LAYERS * depth, total_width)
    residual = block_input.reshape(own_rows, width).astype(f32)
    rows_f32, row_scale, normed = norm_in(residual, attend_gain[0])
    (weights,) = exchange(0, "dp", [packed])
    weights = jnp.moveaxis(weights.reshape(dp, LAYERS, depth, total_width), 1, 0)
    weights = weights.reshape(LAYERS, width, total_width)
    attend_all, normed_all = exchange(
        1, "mp", [weights[:, :, :aw].reshape(LAYERS * width, aw), normed]
    )
    attend_all = attend_all.reshape(mp, LAYERS, width, aw)
    attend_full, feed_full = ([], [])
    for layer in range(LAYERS):
        part = attend_all[:, layer]
        attend_full.append(
            (
                columns_over(part[:, :, :qw]),
                columns_over(part[:, :, qw : qw + kw]),
                columns_over(part[:, :, qw + kw : qw + 2 * kw]),
                columns_over(part[:, :, qw + 2 * kw :]),
            )
        )
        feed = weights[layer, :, aw:]
        feed_full.append((feed[:, :ff], feed[:, ff : 2 * ff], feed[:, 2 * ff :]))

    seg_ids = segments[0]
    positions = doc_positions(seg_ids)
    my_segs = lax.dynamic_slice_in_dim(seg_ids, first_row, own_rows, 0)
    cos_all, sin_all = rope_tables(positions)
    cosine = lax.dynamic_slice_in_dim(cos_all, first_row, own_rows, 0)
    sine = lax.dynamic_slice_in_dim(sin_all, first_row, own_rows, 0)
    key_index = jnp.arange(row_count, dtype=jnp.int32)
    query_index = first_row + jnp.arange(own_rows, dtype=jnp.int32)
    allowed = (key_index[None, :] <= query_index[:, None]) & (seg_ids[None, :] == my_segs[:, None])

    attend_saved = []
    feed_saved = []
    for layer in range(LAYERS):
        query_full, key_full, value_full, mix_turned = attend_full[layer]
        if layer > 0:
            rows_f32, row_scale, normed = norm_in(residual, attend_gain[layer])
            (normed_all,) = exchange(10 + layer, "mp", [normed])
        normed_all = normed_all.reshape(row_count, width)
        query_rows = matmul_f32(normed, query_full).astype(bf16).astype(f32)
        key_rows = matmul_f32(normed_all, key_full).astype(bf16).astype(f32)
        values_all = matmul_f32(normed_all, value_full).astype(bf16)
        query_turned = rotate(query_rows.reshape(own_rows, HEADS, HEAD_DIM), cosine, sine)
        query_turned = query_turned.reshape(own_rows, -1).astype(bf16)
        keys_all = rotate(key_rows.reshape(row_count, KV_HEADS, HEAD_DIM), cos_all, sin_all)
        keys_all = keys_all.reshape(row_count, -1).astype(bf16)
        mixed, log_total = attend(query_turned, keys_all, values_all, allowed)
        mixed = mixed.astype(bf16)
        residual = residual + inner_cols(mixed, mix_turned)
        attend_saved.append(
            (
                rows_f32,
                row_scale,
                normed_all,
                query_turned,
                keys_all,
                values_all,
                log_total,
                mixed,
            )
        )
        rows_two, scale_two, normed_two = norm_in(residual, feed_gain[layer])
        (normed_two,) = exchange(20 + layer, "mp", [normed_two])
        normed_two = normed_two.reshape(row_count, width)
        gate_full, up_full, down_turned = feed_full[layer]
        gate_out = matmul_f32(normed_two, gate_full)
        up_out = matmul_f32(normed_two, up_full)
        hidden = (jax.nn.silu(gate_out) * up_out).astype(bf16)
        part = inner_cols(hidden, down_turned).astype(bf16).reshape(mp, own_rows, width)
        (part,) = exchange(30 + layer, "mp", (), [part])
        residual = residual + summed(part)
        feed_saved.append((rows_two, scale_two, normed_two, gate_out, up_out, hidden))
    block_output = residual.astype(bf16).reshape(own_rows // 2, 2 * width)

    grad_resid = cotangent.reshape(own_rows, width).astype(f32)
    attend_terms = [None] * LAYERS
    feed_terms = [None] * LAYERS
    grads = [None] * LAYERS
    feed_grads = [None] * LAYERS

    def attend_grads(layer, received):
        grad_all, mixed_cols, dqkv_cols = [a.reshape(row_count, -1) for a in received]
        normed_all = attend_saved[layer][2]
        return jnp.concatenate(
            [inner_rows(normed_all, dqkv_cols), inner_rows(grad_all, mixed_cols)], axis=1
        )

    late = None
    for layer in range(LAYERS - 1, -1, -1):
        rows_two, scale_two, normed_two, gate_out, up_out, hidden = feed_saved[layer]
        gate_full, up_full, down_turned = feed_full[layer]
        got = exchange(
            40 + layer,
            "mp",
            [grad_resid.astype(bf16)] + ([late[0]] if late else []),
            late[1:] if late else [],
        )
        grad_full = got[0].reshape(row_count, width)
        if late:
            grads[layer + 1] = attend_grads(layer + 1, got[1:])
        grad_hidden = matmul_f32(grad_full, down_turned)
        down_term = inner_rows(grad_full, hidden)
        sigmoid_gate = jax.nn.sigmoid(gate_out)
        grad_gate = (
            grad_hidden * up_out * sigmoid_gate * (1.0 + gate_out * (1.0 - sigmoid_gate))
        ).astype(bf16)
        grad_up = (grad_hidden * gate_out * sigmoid_gate).astype(bf16)
        grad_normed = (inner_cols(grad_gate, gate_full) + inner_cols(grad_up, up_full)).astype(bf16)
        (part,) = exchange(50 + layer, "mp", (), [grad_normed.reshape(mp, own_rows, width)])
        feed_grads[layer] = jnp.concatenate(
            [inner_rows(normed_two, grad_gate), inner_rows(normed_two, grad_up), down_term], axis=1
        )
        resid_grad, feed_terms[layer] = norm_back(
            summed(part), rows_two, scale_two, feed_gain[layer]
        )
        grad_resid = grad_resid + resid_grad
        (
            rows_f32,
            row_scale,
            normed_all,
            query_turned,
            keys_all,
            values_all,
            log_total,
            mixed,
        ) = attend_saved[layer]
        query_full, key_full, value_full, mix_turned = attend_full[layer]
        grad_low = grad_resid.astype(bf16)
        grad_mixed = matmul_f32(grad_low, mix_turned).astype(bf16)
        grad_query, grad_keys, grad_values = attend_back(
            query_turned, keys_all, values_all, allowed, log_total, grad_mixed
        )
        key_value = jnp.concatenate([grad_keys, grad_values], axis=1).astype(bf16)
        (key_value,) = exchange(
            60 + layer, "mp", (), [key_value.reshape(mp, own_rows, 2 * mp * kw)]
        )
        key_value = summed(key_value)
        query_back = rotate(grad_query.reshape(own_rows, HEADS, HEAD_DIM), cosine, -sine)
        query_back = query_back.reshape(own_rows, -1).astype(bf16)
        key_back = rotate(
            key_value[:, : mp * kw].reshape(own_rows, KV_HEADS, HEAD_DIM), cosine, -sine
        )
        key_back = key_back.reshape(own_rows, -1).astype(bf16)
        value_back = key_value[:, mp * kw :].astype(bf16)
        grad_normed = (
            inner_cols(query_back, query_full)
            + inner_cols(key_back, key_full)
            + inner_cols(value_back, value_full)
        )
        resid_grad, attend_terms[layer] = norm_back(
            grad_normed, rows_f32, row_scale, attend_gain[layer]
        )
        grad_resid = grad_resid + resid_grad
        dqkv = jnp.concatenate(
            [a.reshape(own_rows, mp, -1) for a in (query_back, key_back, value_back)], axis=2
        )
        late = (
            grad_low,
            jnp.moveaxis(mixed.reshape(own_rows, mp, qw), 1, 0),
            jnp.moveaxis(dqkv, 1, 0),
        )
    gains = jnp.concatenate([jnp.stack(attend_terms), jnp.stack(feed_terms)], axis=0)
    gains = jnp.concatenate([gains, jnp.zeros((8 - 2 * LAYERS, width), f32)], axis=0)
    got = exchange(2, "mp", [late[0], gains], late[1:])
    grads[0] = attend_grads(0, (got[0], got[2], got[3]))
    gains = summed(got[1])
    grad_pack = jnp.stack(
        [jnp.concatenate([grads[i], feed_grads[i]], axis=1).astype(bf16) for i in range(LAYERS)]
    )
    grad_pack = jnp.moveaxis(grad_pack.reshape(LAYERS, dp, depth, total_width), 1, 0)
    gains, grad_pack = exchange(
        3, "dp", [gains], [grad_pack.reshape(dp, LAYERS * depth, total_width)]
    )
    gains = summed(gains)
    total = summed(grad_pack).reshape(LAYERS, depth, total_width)
    input_grad = grad_resid.reshape(own_rows // 2, 2 * width)
    return (
        block_output,
        input_grad,
        gains[:LAYERS],
        total[:, :, :qw],
        total[:, :, qw : qw + kw],
        total[:, :, qw + kw : qw + 2 * kw],
        jnp.swapaxes(total[:, :, qw + 2 * kw : aw], 1, 2),
        gains[LAYERS : 2 * LAYERS],
        total[:, :, aw : aw + ff],
        total[:, :, aw + ff : aw + 2 * ff],
        jnp.swapaxes(total[:, :, aw + 2 * ff :], 1, 2),
    )


def solution(mesh):
    in_specs = (
        P(("dp", "mp"), None),
        P("dp", None),
        P(),
        P(None, "dp", "mp"),
        P(None, "dp", "mp"),
        P(None, "dp", "mp"),
        P(None, "mp", "dp"),
        P(),
        P(None, "dp", "mp"),
        P(None, "dp", "mp"),
        P(None, "mp", "dp"),
        P(("dp", "mp"), None),
    )
    out_specs = (
        P(("dp", "mp"), None),
        P(("dp", "mp"), None),
        P(),
        P(None, "dp", "mp"),
        P(None, "dp", "mp"),
        P(None, "dp", "mp"),
        P(None, "mp", "dp"),
        P(),
        P(None, "dp", "mp"),
        P(None, "dp", "mp"),
        P(None, "mp", "dp"),
    )
    return jax.shard_map(
        on_device, mesh=mesh, in_specs=in_specs, out_specs=out_specs, check_vma=False
    )
```

```python
import functools
import math

import jax
import jax.numpy as jnp
from jax import lax
from jax.experimental import pallas as pl
from jax.experimental.pallas import tpu as pltpu
from jax.sharding import PartitionSpec as P

HEADS = 9
KV_HEADS = 3
HEAD_DIM = 64
LAYERS = 2


norm_eps = 1e-05
rope_base = 100000.0
masked_value = -1e30


MESH = pl.DeviceIdType.MESH


def greet(devices):
    barrier = pltpu.get_barrier_semaphore()
    for device in devices:
        pl.semaphore_signal(barrier, inc=1, device_id=device, device_id_type=MESH)
    pl.semaphore_wait(barrier, len(devices))


def send(source, target, sems, at, device):
    copy = pltpu.make_async_remote_copy(
        src_ref=source,
        dst_ref=target,
        send_sem=sems[0].at[at],
        recv_sem=sems[1].at[at],
        device_id=device,
        device_id_type=MESH,
    )
    copy.start()
    return copy


def pair_sems(count):
    return [pltpu.SemaphoreType.DMA((count,)), pltpu.SemaphoreType.DMA((count,))]


def call(kernel, number, shapes, scratch, args, name):
    space = pl.BlockSpec(memory_space=pltpu.VMEM)
    return pl.pallas_call(
        kernel,
        out_shape=shapes,
        in_specs=[space] * len(args),
        out_specs=[space] * len(shapes),
        scratch_shapes=scratch,
        compiler_params=pltpu.CompilerParams(
            collective_id=number, has_side_effects=True, vmem_limit_bytes=48 * 1024 * 1024
        ),
        name=name,
    )(*args)


CHUNKS = 2


def model_kernel(n_whole, n_split, n_sum, peers, *refs):
    n_in = n_whole + n_split + n_sum
    ins, refs = refs[:n_in], refs[n_in:]
    outs, refs = refs[:n_in], refs[n_in:]
    from_core, refs = refs[:n_sum], refs[n_sum:]
    for_far, refs = refs[:n_sum], refs[n_sum:]
    from_far, refs = refs[:n_sum], refs[n_sum:]
    whole_near, whole_far, whole_pass = refs[0:2], refs[2:4], refs[4:6]
    split_sems, sum_near, sum_mid, sum_far = refs[6:8], refs[8:10], refs[10:12], refs[12:14]
    local_sem = refs[14]
    me = lax.axis_index("mp")
    chip, core = me // 2, lax.rem(me, 2)
    near = chip * 2 + (1 - core)
    far = (1 - chip) * 2 + core
    cross = (1 - chip) * 2 + (1 - core)
    others = [near, far, cross]
    greet([{"mp": o} for o in (others if n_split else others[:2])])
    ready, waits = ([], [])
    first_sum = n_whole + n_split
    mids = []
    for i in range(n_sum):
        rows = outs[first_sum + i].shape[0] // CHUNKS
        for k in range(CHUNKS):
            cut = pl.ds(k * rows, rows)
            at = i * CHUNKS + k
            mids.append(
                send(
                    ins[first_sum + i].at[cross, cut],
                    from_core[i].at[0, cut],
                    sum_mid,
                    at,
                    {"mp": near},
                )
            )
        ready.append(
            send(ins[first_sum + i].at[near], from_core[i].at[1], sum_near, i, {"mp": near})
        )
    passes = []
    for i in range(n_whole):
        rows = ins[i].shape[0] // CHUNKS
        for k in range(CHUNKS):
            cut = pl.ds(k * rows, rows)
            at = i * CHUNKS + k
            passes.append(
                send(ins[i].at[cut], outs[i].at[me, cut], whole_far, at, {"mp": far})
            )
        waits.append(send(ins[i], outs[i].at[me], whole_near, i, {"mp": near}))
        local = pltpu.make_async_copy(ins[i], outs[i].at[me], local_sem.at[i])
        local.start()
        waits.append(local)
    for j in range(n_split):
        i = n_whole + j
        for s, o in enumerate(others):
            waits.append(
                send(ins[i].at[o], outs[i].at[me], split_sems, j * 3 + s, {"mp": o})
            )
        local = pltpu.make_async_copy(ins[i].at[me], outs[i].at[me], local_sem.at[i])
        local.start()
        waits.append(local)
    fars = []
    for i in range(n_sum):
        rows = outs[first_sum + i].shape[0] // CHUNKS
        for k in range(CHUNKS):
            cut = pl.ds(k * rows, rows)
            at = i * CHUNKS + k
            mids[at].wait()
            for_far[i][cut] = (
                ins[first_sum + i][far, cut].astype(jnp.float32)
                + from_core[i][0, cut].astype(jnp.float32)
            ).astype(for_far[i].dtype)
            fars.append(
                send(for_far[i].at[cut], from_far[i].at[cut], sum_far, at, {"mp": far})
            )
    for i in range(n_whole):
        rows = ins[i].shape[0] // CHUNKS
        for k in range(CHUNKS):
            cut = pl.ds(k * rows, rows)
            at = i * CHUNKS + k
            passes[at].wait()
            waits.append(
                send(outs[i].at[far, cut], outs[i].at[far, cut], whole_pass, at, {"mp": near})
            )
    for i in range(n_sum):
        ready[i].wait()
        for k in range(CHUNKS):
            fars[i * CHUNKS + k].wait()
        outs[first_sum + i][...] = (
            ins[first_sum + i][me].astype(jnp.float32)
            + from_core[i][1].astype(jnp.float32)
            + from_far[i][...].astype(jnp.float32)
        )
    for copy in waits:
        copy.wait()


def exchange(number, whole=(), split=(), sums=()):
    peers = lax.axis_size("mp")
    args = [*whole, *split, *sums]
    shapes = [jax.ShapeDtypeStruct((peers, *a.shape), a.dtype) for a in whole]
    shapes += [jax.ShapeDtypeStruct(a.shape, a.dtype) for a in split]
    shapes += [jax.ShapeDtypeStruct(a.shape[1:], jnp.float32) for a in sums]
    scratch = [pltpu.VMEM((2, *a.shape[1:]), a.dtype) for a in sums]
    scratch += [pltpu.VMEM(a.shape[1:], a.dtype) for a in sums] * 2
    n_whole, n_split, n_sum = max(1, len(whole)), max(1, len(split)), max(1, len(sums))
    scratch += pair_sems(n_whole) + pair_sems(n_whole * CHUNKS) + pair_sems(n_whole * CHUNKS)
    scratch += pair_sems(n_split * 3) + pair_sems(n_sum)
    scratch += pair_sems(n_sum * CHUNKS) + pair_sems(n_sum * CHUNKS)
    scratch += [pltpu.SemaphoreType.DMA((n_whole + n_split,))]
    kernel = functools.partial(model_kernel, len(whole), len(split), len(sums), peers)
    return call(kernel, number, shapes, scratch, args, "model_exchange")


def weights_kernel(
    groups,
    rows_ref,
    attend_ref,
    feed_ref,
    rows_out,
    attend_out,
    feed_out,
    zf0,
    zf1,
    za0,
    za1,
    xf0,
    xf1,
    xa0,
    xa1,
    y0,
    y1,
    c0,
    c1,
    n0,
    n1,
    local_sem,
):
    zf, za, xf, xa, ys, cs, ns = (
        (zf0, zf1), (za0, za1), (xf0, xf1), (xa0, xa1), (y0, y1), (c0, c1), (n0, n1)
    )
    me, index = lax.axis_index("mp"), lax.axis_index("dp")
    chip, core = me // 2, lax.rem(me, 2)
    near = {"mp": chip * 2 + (1 - core)}
    far_index = (1 - chip) * 2 + core
    far = {"mp": far_index}
    group, side = index // 2, lax.rem(index, 2)
    beside = {"dp": group * 2 + (1 - side)}
    line = [{"dp": lax.rem(group + s, groups) * 2 + side} for s in range(1, groups)]
    greet([near, far, beside, *line])
    waits = []
    to_line, to_beside, to_far = ([], [], [])
    n_far = send(rows_ref, rows_out.at[me], ns, 0, far)
    waits.append(send(rows_ref, rows_out.at[me], ns, 1, near))
    for s in range(1, groups):
        to_line.append(
            (
                send(attend_ref, attend_out.at[me, index], za, s, line[s - 1]),
                send(feed_ref, feed_out.at[index], zf, s, line[s - 1]),
            )
        )
    to_beside.append(send(attend_ref, attend_out.at[me, index], xa, 0, beside))
    waits.append(send(feed_ref, feed_out.at[index], xf, 0, beside))
    to_far.append((index, send(attend_ref, attend_out.at[me, index], ys, 0, far)))
    waits.append(send(attend_ref, attend_out.at[me, index], cs, 0, near))
    for i, (a, o) in enumerate(
        (
            (rows_ref, rows_out.at[me]),
            (attend_ref, attend_out.at[me, index]),
            (feed_ref, feed_out.at[index]),
        )
    ):
        local = pltpu.make_async_copy(a, o, local_sem.at[i])
        local.start()
        waits.append(local)
    n_far.wait()
    waits.append(send(rows_out.at[far_index], rows_out.at[far_index], ns, 2, near))

    def share(at, block):
        to_far.append(
            (block, send(attend_out.at[me, block], attend_out.at[me, block], ys, at, far))
        )
        waits.append(send(attend_out.at[me, block], attend_out.at[me, block], cs, at, near))

    def pass_on(at):
        block, copy = to_far[at]
        copy.wait()
        waits.append(
            send(
                attend_out.at[far_index, block],
                attend_out.at[far_index, block],
                cs,
                2 * groups + at,
                near,
            )
        )

    for s in range(1, groups):
        block = lax.rem(group + groups - s, groups) * 2 + side
        to_line[s - 1][0].wait()
        to_beside.append(
            send(attend_out.at[me, block], attend_out.at[me, block], xa, s, beside)
        )
        share(s, block)
        to_line[s - 1][1].wait()
        waits.append(send(feed_out.at[block], feed_out.at[block], xf, s, beside))
        pass_on(s - 1)
    for s in range(groups):
        block = lax.rem(group + groups - s, groups) * 2 + (1 - side)
        to_beside[s].wait()
        share(groups + s, block)
        pass_on(groups - 1 + s)
    pass_on(2 * groups - 1)
    for copy in waits:
        copy.wait()


def gather_weights(number, rows, attend, feed):
    mp, dp = lax.axis_size("mp"), lax.axis_size("dp")
    groups = dp // 2
    shapes = [
        jax.ShapeDtypeStruct((mp, *rows.shape), rows.dtype),
        jax.ShapeDtypeStruct((mp, dp, *attend.shape), attend.dtype),
        jax.ShapeDtypeStruct((dp, *feed.shape), feed.dtype),
    ]
    scratch = pair_sems(groups) * 4 + pair_sems(2 * groups) + pair_sems(4 * groups) + pair_sems(3)
    scratch += [pltpu.SemaphoreType.DMA((3,))]
    kernel = functools.partial(weights_kernel, groups)
    return call(kernel, number, shapes, scratch, (rows, attend, feed), "gather_weights")


def grads_kernel(
    groups,
    grad_ref,
    gain_ref,
    grad_out,
    gain_out,
    x_in,
    z_send,
    z_in,
    gain_x,
    gain_send,
    gain_z,
    x0,
    x1,
    z0,
    z1,
    gx0,
    gx1,
    gz0,
    gz1,
):
    xs, zs, gx, gz = (x0, x1), (z0, z1), (gx0, gx1), (gz0, gz1)
    index = lax.axis_index("dp")
    group, side = index // 2, lax.rem(index, 2)
    beside = {"dp": group * 2 + (1 - side)}
    line = [lax.rem(group + s, groups) for s in range(groups)]
    greet([beside] + [{"dp": g * 2 + side} for g in line[1:]])
    order = [*range(1, groups), 0]
    gain_copy = send(gain_ref, gain_x, gx, 0, beside)
    copies = {
        s: send(grad_ref.at[line[s] * 2 + (1 - side)], x_in.at[s], xs, s, beside) for s in order
    }
    gain_copy.wait()
    gain_send[...] = gain_ref[...] + gain_x[...]
    later = []
    for s in range(1, groups):
        device = {"dp": line[s] * 2 + side}
        gain_copy = send(gain_send, gain_z.at[s], gz, s, device)
        copies[s].wait()
        z_send[s] = (
            grad_ref[line[s] * 2 + side].astype(jnp.float32) + x_in[s].astype(jnp.float32)
        ).astype(z_send.dtype)
        later.append((send(z_send.at[s], z_in.at[s], zs, s, device), gain_copy))
    copies[0].wait()
    grad_out[...] = grad_ref[index].astype(jnp.float32) + x_in[0].astype(jnp.float32)
    gain_out[...] = gain_send[...]
    for s in range(1, groups):
        later[s - 1][1].wait()
        gain_out[...] += gain_z[s]
        later[s - 1][0].wait()
        grad_out[...] += z_in[s].astype(jnp.float32)


def sum_grads(number, grad_pack, gains):
    dp = lax.axis_size("dp")
    groups = dp // 2
    block = grad_pack.shape[1:]
    shapes = [
        jax.ShapeDtypeStruct(block, jnp.float32),
        jax.ShapeDtypeStruct(gains.shape, jnp.float32),
    ]
    scratch = [pltpu.VMEM((groups, *block), grad_pack.dtype)] * 3
    scratch += [pltpu.VMEM(gains.shape, jnp.float32)] * 2
    scratch += [pltpu.VMEM((groups, *gains.shape), jnp.float32)]
    scratch += pair_sems(groups) * 2 + pair_sems(1) + pair_sems(groups)
    kernel = functools.partial(grads_kernel, groups)
    return call(kernel, number, shapes, scratch, (grad_pack, gains), "sum_grads")


def doc_positions(seg_ids):
    length_all = seg_ids.shape[-1]
    token_index = jnp.arange(length_all, dtype=jnp.int32)
    starts = jnp.concatenate(
        [token_index[..., :1] == 0, seg_ids[..., 1:] != seg_ids[..., :-1]], axis=-1
    )
    doc_start = lax.cummax(jnp.where(starts, token_index, 0), axis=seg_ids.ndim - 1)
    return token_index - doc_start


def rope_tables(positions):
    half_dim = HEAD_DIM // 2
    exponents = jnp.arange(half_dim, dtype=jnp.float32) * (2.0 / HEAD_DIM)
    inverse = jnp.exp(-math.log(rope_base) * exponents)
    angles = positions.astype(jnp.float32)[..., None] * inverse
    cosine = jnp.cos(angles)
    sine = jnp.sin(angles)
    return (jnp.concatenate([cosine, cosine], axis=-1), jnp.concatenate([sine, sine], axis=-1))


def rotate(values, cosine, sine):
    half_dim = values.shape[-1] // 2
    turned = jnp.concatenate([-values[..., half_dim:], values[..., :half_dim]], axis=-1)
    return values * cosine[..., None, :] + turned * sine[..., None, :]


def matmul_f32(left, right):
    return jnp.dot(left, right, preferred_element_type=jnp.float32)


def inner_rows(left, right):
    return lax.dot_general(
        left, right, (((0,), (0,)), ((), ())), preferred_element_type=jnp.float32
    )


def inner_cols(left, right):
    return lax.dot_general(
        left, right, (((1,), (1,)), ((), ())), preferred_element_type=jnp.float32
    )


def norm_in(residual, gain):
    rows_f32 = residual.astype(jnp.bfloat16).astype(jnp.float32)
    row_scale = lax.rsqrt(jnp.mean(rows_f32 * rows_f32, axis=1, keepdims=True) + norm_eps)
    normed = (rows_f32 * row_scale * gain.astype(jnp.float32)).astype(jnp.bfloat16)
    return (rows_f32, row_scale, normed)


def summed(pieces):
    return jnp.sum(pieces.astype(jnp.float32), axis=0)


def columns_over(gathered):
    peers, rows, width = gathered.shape
    return jnp.moveaxis(gathered, 0, 1).reshape(rows, peers * width)


def norm_back(grad_normed, rows_f32, row_scale, gain):
    width = rows_f32.shape[1]
    gain_f32 = gain.astype(jnp.float32)
    cubed = row_scale * row_scale * row_scale
    inner = jnp.sum(grad_normed * gain_f32 * rows_f32, axis=1, keepdims=True)
    resid_grad = gain_f32 * row_scale * grad_normed - rows_f32 * cubed * inner / width
    gain_term = jnp.sum(grad_normed * rows_f32 * row_scale, axis=0)
    return (resid_grad, gain_term)


def head_views(query_turned, keys_all, values_all):
    own_rows = query_turned.shape[0]
    group_size = HEADS // KV_HEADS
    query_heads = query_turned.reshape(own_rows, KV_HEADS, group_size, HEAD_DIM)
    key_heads = keys_all.reshape(keys_all.shape[0], KV_HEADS, HEAD_DIM)
    value_heads = values_all.reshape(values_all.shape[0], KV_HEADS, HEAD_DIM)
    return (query_heads, key_heads, value_heads)


def masked_logits(query_heads, key_heads, allowed):
    scores = jnp.einsum(
        "qkgd,tkd->kgqt", query_heads, key_heads, preferred_element_type=jnp.float32
    )
    return jnp.where(allowed, scores * (1.0 / math.sqrt(HEAD_DIM)), masked_value)


def attend(query_turned, keys_all, values_all, allowed):
    query_heads, key_heads, value_heads = head_views(query_turned, keys_all, values_all)
    logits = masked_logits(query_heads, key_heads, allowed)
    row_max = jnp.max(logits, axis=3, keepdims=True)
    raised = jnp.exp(logits - row_max)
    row_total = jnp.sum(raised, axis=3, keepdims=True)
    weights_low = (raised / row_total).astype(jnp.bfloat16)
    mixed = jnp.einsum(
        "kgqt,tkd->qkgd", weights_low, value_heads, preferred_element_type=jnp.float32
    )
    return (mixed.reshape(query_turned.shape[0], -1), row_max + jnp.log(row_total))


def attend_back(query_turned, keys_all, values_all, allowed, log_total, grad_mixed):
    query_heads, key_heads, value_heads = head_views(query_turned, keys_all, values_all)
    logits = masked_logits(query_heads, key_heads, allowed)
    weights = jnp.exp(logits - log_total)
    grad_heads = grad_mixed.reshape(query_heads.shape)
    grad_weights = jnp.einsum(
        "qkgd,tkd->kgqt", grad_heads, value_heads, preferred_element_type=jnp.float32
    )
    delta = jnp.sum(weights * grad_weights, axis=3, keepdims=True)
    grad_scores = (weights * (grad_weights - delta) * (1.0 / math.sqrt(HEAD_DIM))).astype(
        jnp.bfloat16
    )
    grad_query = jnp.einsum(
        "kgqt,tkd->qkgd", grad_scores, key_heads, preferred_element_type=jnp.float32
    )
    grad_keys = jnp.einsum(
        "kgqt,qkgd->tkd", grad_scores, query_heads, preferred_element_type=jnp.float32
    )
    grad_values = jnp.einsum(
        "kgqt,qkgd->tkd",
        weights.astype(jnp.bfloat16),
        grad_heads,
        preferred_element_type=jnp.float32,
    )
    row_count = keys_all.shape[0]
    return (
        grad_query.reshape(query_turned.shape[0], -1),
        grad_keys.reshape(row_count, -1),
        grad_values.reshape(row_count, -1),
    )


def on_device(
    block_input,
    segments,
    attend_gain,
    query_weight,
    key_weight,
    value_weight,
    mix_weight,
    feed_gain,
    gate_weight,
    up_weight,
    down_weight,
    cotangent,
):
    bf16, f32 = jnp.bfloat16, jnp.float32
    width = block_input.shape[1] // 2
    own_rows = block_input.shape[0] * 2
    mp = lax.axis_size("mp")
    dp = lax.axis_size("dp")
    row_count = own_rows * mp
    first_row = lax.axis_index("mp") * own_rows
    qw, kw, ff = query_weight.shape[2], key_weight.shape[2], gate_weight.shape[2]
    depth = query_weight.shape[1]
    aw = 2 * qw + 2 * kw
    packed = jnp.concatenate(
        [
            query_weight,
            key_weight,
            value_weight,
            jnp.swapaxes(mix_weight, 1, 2),
            gate_weight,
            up_weight,
            jnp.swapaxes(down_weight, 1, 2),
        ],
        axis=2,
    )
    total_width = packed.shape[2]
    packed = packed.reshape(LAYERS * depth, total_width)
    residual = block_input.reshape(own_rows, width).astype(f32)
    rows_f32, row_scale, normed = norm_in(residual, attend_gain[0])
    normed_all, attend_all, feed_all = gather_weights(0, normed, packed[:, :aw], packed[:, aw:])
    attend_all = jnp.moveaxis(attend_all.reshape(mp, dp, LAYERS, depth, aw), 2, 1)
    attend_all = attend_all.reshape(mp, LAYERS, width, aw)
    feed_all = jnp.moveaxis(feed_all.reshape(dp, LAYERS, depth, total_width - aw), 1, 0)
    feed_all = feed_all.reshape(LAYERS, width, total_width - aw)
    attend_full, feed_full = ([], [])
    for layer in range(LAYERS):
        part = attend_all[:, layer]
        attend_full.append(
            (
                columns_over(part[:, :, :qw]),
                columns_over(part[:, :, qw : qw + kw]),
                columns_over(part[:, :, qw + kw : qw + 2 * kw]),
                columns_over(part[:, :, qw + 2 * kw :]),
            )
        )
        feed = feed_all[layer]
        feed_full.append((feed[:, :ff], feed[:, ff : 2 * ff], feed[:, 2 * ff :]))

    seg_ids = segments[0]
    positions = doc_positions(seg_ids)
    my_segs = lax.dynamic_slice_in_dim(seg_ids, first_row, own_rows, 0)
    cos_all, sin_all = rope_tables(positions)
    cosine = lax.dynamic_slice_in_dim(cos_all, first_row, own_rows, 0)
    sine = lax.dynamic_slice_in_dim(sin_all, first_row, own_rows, 0)
    key_index = jnp.arange(row_count, dtype=jnp.int32)
    query_index = first_row + jnp.arange(own_rows, dtype=jnp.int32)
    allowed = (key_index[None, :] <= query_index[:, None]) & (seg_ids[None, :] == my_segs[:, None])

    attend_saved = []
    feed_saved = []
    for layer in range(LAYERS):
        query_full, key_full, value_full, mix_turned = attend_full[layer]
        if layer > 0:
            rows_f32, row_scale, normed = norm_in(residual, attend_gain[layer])
            (normed_all,) = exchange(10 + layer, [normed])
        normed_all = normed_all.reshape(row_count, width)
        query_rows = matmul_f32(normed, query_full).astype(bf16).astype(f32)
        key_rows = matmul_f32(normed_all, key_full).astype(bf16).astype(f32)
        values_all = matmul_f32(normed_all, value_full).astype(bf16)
        query_turned = rotate(query_rows.reshape(own_rows, HEADS, HEAD_DIM), cosine, sine)
        query_turned = query_turned.reshape(own_rows, -1).astype(bf16)
        keys_all = rotate(key_rows.reshape(row_count, KV_HEADS, HEAD_DIM), cos_all, sin_all)
        keys_all = keys_all.reshape(row_count, -1).astype(bf16)
        mixed, log_total = attend(query_turned, keys_all, values_all, allowed)
        mixed = mixed.astype(bf16)
        residual = residual + inner_cols(mixed, mix_turned)
        attend_saved.append(
            (
                rows_f32,
                row_scale,
                normed_all,
                query_turned,
                keys_all,
                values_all,
                log_total,
                mixed,
            )
        )
        rows_two, scale_two, normed_two = norm_in(residual, feed_gain[layer])
        (normed_two,) = exchange(20 + layer, [normed_two])
        normed_two = normed_two.reshape(row_count, width)
        gate_full, up_full, down_turned = feed_full[layer]
        gate_out = matmul_f32(normed_two, gate_full)
        up_out = matmul_f32(normed_two, up_full)
        hidden = (jax.nn.silu(gate_out) * up_out).astype(bf16)
        part = inner_cols(hidden, down_turned).astype(bf16).reshape(mp, own_rows, width)
        (part,) = exchange(30 + layer, (), (), [part])
        residual = residual + part
        feed_saved.append((rows_two, scale_two, normed_two, gate_out, up_out, hidden))
    block_output = residual.astype(bf16).reshape(own_rows // 2, 2 * width)

    grad_resid = cotangent.reshape(own_rows, width).astype(f32)
    attend_terms = [None] * LAYERS
    feed_terms = [None] * LAYERS
    grads = [None] * LAYERS
    feed_grads = [None] * LAYERS

    def attend_grads(layer, received):
        grad_all, mixed_cols, dqkv_cols = [a.reshape(row_count, -1) for a in received]
        normed_all = attend_saved[layer][2]
        return jnp.concatenate(
            [inner_rows(normed_all, dqkv_cols), inner_rows(grad_all, mixed_cols)], axis=1
        )

    late = None
    for layer in range(LAYERS - 1, -1, -1):
        rows_two, scale_two, normed_two, gate_out, up_out, hidden = feed_saved[layer]
        gate_full, up_full, down_turned = feed_full[layer]
        got = exchange(
            40 + layer,
            [grad_resid.astype(bf16)] + ([late[0]] if late else []),
            late[1:] if late else [],
        )
        grad_full = got[0].reshape(row_count, width)
        if late:
            grads[layer + 1] = attend_grads(layer + 1, got[1:])
        grad_hidden = matmul_f32(grad_full, down_turned)
        down_term = inner_rows(grad_full, hidden)
        sigmoid_gate = jax.nn.sigmoid(gate_out)
        grad_gate = (
            grad_hidden * up_out * sigmoid_gate * (1.0 + gate_out * (1.0 - sigmoid_gate))
        ).astype(bf16)
        grad_up = (grad_hidden * gate_out * sigmoid_gate).astype(bf16)
        grad_normed = (inner_cols(grad_gate, gate_full) + inner_cols(grad_up, up_full)).astype(bf16)
        (part,) = exchange(50 + layer, (), (), [grad_normed.reshape(mp, own_rows, width)])
        feed_grads[layer] = jnp.concatenate(
            [inner_rows(normed_two, grad_gate), inner_rows(normed_two, grad_up), down_term], axis=1
        )
        resid_grad, feed_terms[layer] = norm_back(
            part, rows_two, scale_two, feed_gain[layer]
        )
        grad_resid = grad_resid + resid_grad
        (
            rows_f32,
            row_scale,
            normed_all,
            query_turned,
            keys_all,
            values_all,
            log_total,
            mixed,
        ) = attend_saved[layer]
        query_full, key_full, value_full, mix_turned = attend_full[layer]
        grad_low = grad_resid.astype(bf16)
        grad_mixed = matmul_f32(grad_low, mix_turned).astype(bf16)
        grad_query, grad_keys, grad_values = attend_back(
            query_turned, keys_all, values_all, allowed, log_total, grad_mixed
        )
        key_value = jnp.concatenate([grad_keys, grad_values], axis=1).astype(bf16)
        (key_value,) = exchange(
            60 + layer, (), (), [key_value.reshape(mp, own_rows, 2 * mp * kw)]
        )
        query_back = rotate(grad_query.reshape(own_rows, HEADS, HEAD_DIM), cosine, -sine)
        query_back = query_back.reshape(own_rows, -1).astype(bf16)
        key_back = rotate(
            key_value[:, : mp * kw].reshape(own_rows, KV_HEADS, HEAD_DIM), cosine, -sine
        )
        key_back = key_back.reshape(own_rows, -1).astype(bf16)
        value_back = key_value[:, mp * kw :].astype(bf16)
        grad_normed = (
            inner_cols(query_back, query_full)
            + inner_cols(key_back, key_full)
            + inner_cols(value_back, value_full)
        )
        resid_grad, attend_terms[layer] = norm_back(
            grad_normed, rows_f32, row_scale, attend_gain[layer]
        )
        grad_resid = grad_resid + resid_grad
        dqkv = jnp.concatenate(
            [a.reshape(own_rows, mp, -1) for a in (query_back, key_back, value_back)], axis=2
        )
        late = (
            grad_low,
            jnp.moveaxis(mixed.reshape(own_rows, mp, qw), 1, 0),
            jnp.moveaxis(dqkv, 1, 0),
        )
    gains = jnp.concatenate([jnp.stack(attend_terms), jnp.stack(feed_terms)], axis=0)
    gains = jnp.concatenate([gains, jnp.zeros((16 - 2 * LAYERS, width), f32)], axis=0)
    got = exchange(2, [late[0], gains], late[1:])
    grads[0] = attend_grads(0, (got[0], got[2], got[3]))
    gains = summed(got[1])
    grad_pack = jnp.stack(
        [jnp.concatenate([grads[i], feed_grads[i]], axis=1).astype(bf16) for i in range(LAYERS)]
    )
    grad_pack = jnp.moveaxis(grad_pack.reshape(LAYERS, dp, depth, total_width), 1, 0)
    total, gains = sum_grads(3, grad_pack.reshape(dp, LAYERS * depth, total_width), gains)
    total = total.reshape(LAYERS, depth, total_width)
    input_grad = grad_resid.reshape(own_rows // 2, 2 * width)
    return (
        block_output,
        input_grad,
        gains[:LAYERS],
        total[:, :, :qw],
        total[:, :, qw : qw + kw],
        total[:, :, qw + kw : qw + 2 * kw],
        jnp.swapaxes(total[:, :, qw + 2 * kw : aw], 1, 2),
        gains[LAYERS : 2 * LAYERS],
        total[:, :, aw : aw + ff],
        total[:, :, aw + ff : aw + 2 * ff],
        jnp.swapaxes(total[:, :, aw + 2 * ff :], 1, 2),
    )


def solution(mesh):
    in_specs = (
        P(("dp", "mp"), None),
        P("dp", None),
        P(),
        P(None, "dp", "mp"),
        P(None, "dp", "mp"),
        P(None, "dp", "mp"),
        P(None, "mp", "dp"),
        P(),
        P(None, "dp", "mp"),
        P(None, "dp", "mp"),
        P(None, "mp", "dp"),
        P(("dp", "mp"), None),
    )
    out_specs = (
        P(("dp", "mp"), None),
        P(("dp", "mp"), None),
        P(),
        P(None, "dp", "mp"),
        P(None, "dp", "mp"),
        P(None, "dp", "mp"),
        P(None, "mp", "dp"),
        P(),
        P(None, "dp", "mp"),
        P(None, "dp", "mp"),
        P(None, "mp", "dp"),
    )
    return jax.shard_map(
        on_device, mesh=mesh, in_specs=in_specs, out_specs=out_specs, check_vma=False
    )
```

```python
import functools
import math

import jax
import jax.numpy as jnp
from jax import lax
from jax.experimental import pallas as pl
from jax.experimental.pallas import tpu as pltpu
from jax.sharding import PartitionSpec as P

HEADS = 9
KV_HEADS = 3
HEAD_DIM = 64
LAYERS = 2


norm_eps = 1e-05
rope_base = 100000.0
masked_value = -1e30


MESH = pl.DeviceIdType.MESH


def greet(devices):
    barrier = pltpu.get_barrier_semaphore()
    for device in devices:
        pl.semaphore_signal(barrier, inc=1, device_id=device, device_id_type=MESH)
    pl.semaphore_wait(barrier, len(devices))


def send(source, target, sems, at, device):
    copy = pltpu.make_async_remote_copy(
        src_ref=source,
        dst_ref=target,
        send_sem=sems[0].at[at],
        recv_sem=sems[1].at[at],
        device_id=device,
        device_id_type=MESH,
    )
    copy.start()
    return copy


def pair_sems(count):
    return [pltpu.SemaphoreType.DMA((count,)), pltpu.SemaphoreType.DMA((count,))]


def call(kernel, number, shapes, scratch, args, name):
    space = pl.BlockSpec(memory_space=pltpu.VMEM)
    return pl.pallas_call(
        kernel,
        out_shape=shapes,
        in_specs=[space] * len(args),
        out_specs=[space] * len(shapes),
        scratch_shapes=scratch,
        compiler_params=pltpu.CompilerParams(
            collective_id=number, has_side_effects=True, vmem_limit_bytes=48 * 1024 * 1024
        ),
        name=name,
    )(*args)


CHUNKS = 2


def model_kernel(n_whole, n_split, n_sum, peers, *refs):
    n_in = n_whole + n_split + n_sum
    ins, refs = refs[:n_in], refs[n_in:]
    outs, refs = refs[:n_in], refs[n_in:]
    from_core, refs = refs[:n_sum], refs[n_sum:]
    for_far, refs = refs[:n_sum], refs[n_sum:]
    from_far, refs = refs[:n_sum], refs[n_sum:]
    whole_near, whole_far, whole_pass = refs[0:2], refs[2:4], refs[4:6]
    split_sems, sum_near, sum_mid, sum_far = refs[6:8], refs[8:10], refs[10:12], refs[12:14]
    local_sem = refs[14]
    me = lax.axis_index("mp")
    chip, core = me // 2, lax.rem(me, 2)
    near = chip * 2 + (1 - core)
    far = (1 - chip) * 2 + core
    cross = (1 - chip) * 2 + (1 - core)
    others = [near, far, cross]
    greet([{"mp": o} for o in (others if n_split else others[:2])])
    ready, waits = ([], [])
    first_sum = n_whole + n_split
    mids = []
    for i in range(n_sum):
        rows = outs[first_sum + i].shape[0] // CHUNKS
        for k in range(CHUNKS):
            cut = pl.ds(k * rows, rows)
            at = i * CHUNKS + k
            mids.append(
                send(
                    ins[first_sum + i].at[cross, cut],
                    from_core[i].at[0, cut],
                    sum_mid,
                    at,
                    {"mp": near},
                )
            )
        ready.append(
            send(ins[first_sum + i].at[near], from_core[i].at[1], sum_near, i, {"mp": near})
        )
    passes = []
    for i in range(n_whole):
        rows = ins[i].shape[0] // CHUNKS
        for k in range(CHUNKS):
            cut = pl.ds(k * rows, rows)
            at = i * CHUNKS + k
            passes.append(
                send(ins[i].at[cut], outs[i].at[me, cut], whole_far, at, {"mp": far})
            )
        waits.append(send(ins[i], outs[i].at[me], whole_near, i, {"mp": near}))
        local = pltpu.make_async_copy(ins[i], outs[i].at[me], local_sem.at[i])
        local.start()
        waits.append(local)
    for j in range(n_split):
        i = n_whole + j
        for s, o in enumerate(others):
            waits.append(
                send(ins[i].at[o], outs[i].at[me], split_sems, j * 3 + s, {"mp": o})
            )
        local = pltpu.make_async_copy(ins[i].at[me], outs[i].at[me], local_sem.at[i])
        local.start()
        waits.append(local)
    fars = []
    for i in range(n_sum):
        rows = outs[first_sum + i].shape[0] // CHUNKS
        for k in range(CHUNKS):
            cut = pl.ds(k * rows, rows)
            at = i * CHUNKS + k
            mids[at].wait()
            for_far[i][cut] = (
                ins[first_sum + i][far, cut].astype(jnp.float32)
                + from_core[i][0, cut].astype(jnp.float32)
            ).astype(for_far[i].dtype)
            fars.append(
                send(for_far[i].at[cut], from_far[i].at[cut], sum_far, at, {"mp": far})
            )
    for i in range(n_whole):
        rows = ins[i].shape[0] // CHUNKS
        for k in range(CHUNKS):
            cut = pl.ds(k * rows, rows)
            at = i * CHUNKS + k
            passes[at].wait()
            waits.append(
                send(outs[i].at[far, cut], outs[i].at[far, cut], whole_pass, at, {"mp": near})
            )
    for i in range(n_sum):
        ready[i].wait()
        for k in range(CHUNKS):
            fars[i * CHUNKS + k].wait()
        outs[first_sum + i][...] = (
            ins[first_sum + i][me].astype(jnp.float32)
            + from_core[i][1].astype(jnp.float32)
            + from_far[i][...].astype(jnp.float32)
        )
    for copy in waits:
        copy.wait()


def exchange(number, whole=(), split=(), sums=()):
    peers = lax.axis_size("mp")
    args = [*whole, *split, *sums]
    shapes = [jax.ShapeDtypeStruct((peers, *a.shape), a.dtype) for a in whole]
    shapes += [jax.ShapeDtypeStruct(a.shape, a.dtype) for a in split]
    shapes += [jax.ShapeDtypeStruct(a.shape[1:], jnp.float32) for a in sums]
    scratch = [pltpu.VMEM((2, *a.shape[1:]), a.dtype) for a in sums]
    scratch += [pltpu.VMEM(a.shape[1:], a.dtype) for a in sums] * 2
    n_whole, n_split, n_sum = max(1, len(whole)), max(1, len(split)), max(1, len(sums))
    scratch += pair_sems(n_whole) + pair_sems(n_whole * CHUNKS) + pair_sems(n_whole * CHUNKS)
    scratch += pair_sems(n_split * 3) + pair_sems(n_sum)
    scratch += pair_sems(n_sum * CHUNKS) + pair_sems(n_sum * CHUNKS)
    scratch += [pltpu.SemaphoreType.DMA((n_whole + n_split,))]
    kernel = functools.partial(model_kernel, len(whole), len(split), len(sums), peers)
    return call(kernel, number, shapes, scratch, args, "model_exchange")


def weights_kernel(
    groups,
    rows_ref,
    attend_ref,
    feed_ref,
    rows_out,
    attend_out,
    feed_out,
    zf0,
    zf1,
    za0,
    za1,
    xf0,
    xf1,
    xa0,
    xa1,
    y0,
    y1,
    c0,
    c1,
    n0,
    n1,
    local_sem,
):
    zf, za, xf, xa, ys, cs, ns = (
        (zf0, zf1), (za0, za1), (xf0, xf1), (xa0, xa1), (y0, y1), (c0, c1), (n0, n1)
    )
    me, index = lax.axis_index("mp"), lax.axis_index("dp")
    chip, core = me // 2, lax.rem(me, 2)
    near = {"mp": chip * 2 + (1 - core)}
    far_index = (1 - chip) * 2 + core
    far = {"mp": far_index}
    group, side = index // 2, lax.rem(index, 2)
    beside = {"dp": group * 2 + (1 - side)}
    line = [{"dp": lax.rem(group + s, groups) * 2 + side} for s in range(1, groups)]
    greet([near, far, beside, *line])
    waits = []
    to_line, to_beside, to_far = ([], [], [])
    n_far = send(rows_ref, rows_out.at[me], ns, 0, far)
    waits.append(send(rows_ref, rows_out.at[me], ns, 1, near))
    for s in range(1, groups):
        to_line.append(
            (
                send(attend_ref, attend_out.at[me, index], za, s, line[s - 1]),
                send(feed_ref, feed_out.at[index], zf, s, line[s - 1]),
            )
        )
    to_beside.append(send(attend_ref, attend_out.at[me, index], xa, 0, beside))
    waits.append(send(feed_ref, feed_out.at[index], xf, 0, beside))
    to_far.append((index, send(attend_ref, attend_out.at[me, index], ys, 0, far)))
    waits.append(send(attend_ref, attend_out.at[me, index], cs, 0, near))
    for i, (a, o) in enumerate(
        (
            (rows_ref, rows_out.at[me]),
            (attend_ref, attend_out.at[me, index]),
            (feed_ref, feed_out.at[index]),
        )
    ):
        local = pltpu.make_async_copy(a, o, local_sem.at[i])
        local.start()
        waits.append(local)
    n_far.wait()
    waits.append(send(rows_out.at[far_index], rows_out.at[far_index], ns, 2, near))

    def share(at, block):
        to_far.append(
            (block, send(attend_out.at[me, block], attend_out.at[me, block], ys, at, far))
        )
        waits.append(send(attend_out.at[me, block], attend_out.at[me, block], cs, at, near))

    def pass_on(at):
        block, copy = to_far[at]
        copy.wait()
        waits.append(
            send(
                attend_out.at[far_index, block],
                attend_out.at[far_index, block],
                cs,
                2 * groups + at,
                near,
            )
        )

    for s in range(1, groups):
        block = lax.rem(group + groups - s, groups) * 2 + side
        to_line[s - 1][0].wait()
        to_beside.append(
            send(attend_out.at[me, block], attend_out.at[me, block], xa, s, beside)
        )
        share(s, block)
        to_line[s - 1][1].wait()
        waits.append(send(feed_out.at[block], feed_out.at[block], xf, s, beside))
        pass_on(s - 1)
    for s in range(groups):
        block = lax.rem(group + groups - s, groups) * 2 + (1 - side)
        to_beside[s].wait()
        share(groups + s, block)
        pass_on(groups - 1 + s)
    pass_on(2 * groups - 1)
    for copy in waits:
        copy.wait()


def gather_weights(number, rows, attend, feed):
    mp, dp = lax.axis_size("mp"), lax.axis_size("dp")
    groups = dp // 2
    shapes = [
        jax.ShapeDtypeStruct((mp, *rows.shape), rows.dtype),
        jax.ShapeDtypeStruct((mp, dp, *attend.shape), attend.dtype),
        jax.ShapeDtypeStruct((dp, *feed.shape), feed.dtype),
    ]
    scratch = pair_sems(groups) * 4 + pair_sems(2 * groups) + pair_sems(4 * groups) + pair_sems(3)
    scratch += [pltpu.SemaphoreType.DMA((3,))]
    kernel = functools.partial(weights_kernel, groups)
    return call(kernel, number, shapes, scratch, (rows, attend, feed), "gather_weights")


def grads_kernel(
    groups,
    grad_ref,
    gain_ref,
    grad_out,
    gain_out,
    x_in,
    z_send,
    z_in,
    gain_x,
    gain_send,
    gain_z,
    x0,
    x1,
    z0,
    z1,
    gx0,
    gx1,
    gz0,
    gz1,
):
    xs, zs, gx, gz = (x0, x1), (z0, z1), (gx0, gx1), (gz0, gz1)
    index = lax.axis_index("dp")
    group, side = index // 2, lax.rem(index, 2)
    beside = {"dp": group * 2 + (1 - side)}
    line = [lax.rem(group + s, groups) for s in range(groups)]
    greet([beside] + [{"dp": g * 2 + side} for g in line[1:]])
    order = [*range(1, groups), 0]
    gain_copy = send(gain_ref, gain_x, gx, 0, beside)
    copies = {
        s: send(grad_ref.at[line[s] * 2 + (1 - side)], x_in.at[s], xs, s, beside) for s in order
    }
    gain_copy.wait()
    gain_send[...] = gain_ref[...] + gain_x[...]
    later = []
    for s in range(1, groups):
        device = {"dp": line[s] * 2 + side}
        gain_copy = send(gain_send, gain_z.at[s], gz, s, device)
        copies[s].wait()
        z_send[s] = (
            grad_ref[line[s] * 2 + side].astype(jnp.float32) + x_in[s].astype(jnp.float32)
        ).astype(z_send.dtype)
        later.append((send(z_send.at[s], z_in.at[s], zs, s, device), gain_copy))
    copies[0].wait()
    grad_out[...] = grad_ref[index].astype(jnp.float32) + x_in[0].astype(jnp.float32)
    gain_out[...] = gain_send[...]
    for s in range(1, groups):
        later[s - 1][1].wait()
        gain_out[...] += gain_z[s]
        later[s - 1][0].wait()
        grad_out[...] += z_in[s].astype(jnp.float32)


def sum_grads(number, grad_pack, gains):
    dp = lax.axis_size("dp")
    groups = dp // 2
    block = grad_pack.shape[1:]
    shapes = [
        jax.ShapeDtypeStruct(block, jnp.float32),
        jax.ShapeDtypeStruct(gains.shape, jnp.float32),
    ]
    scratch = [pltpu.VMEM((groups, *block), grad_pack.dtype)] * 3
    scratch += [pltpu.VMEM(gains.shape, jnp.float32)] * 2
    scratch += [pltpu.VMEM((groups, *gains.shape), jnp.float32)]
    scratch += pair_sems(groups) * 2 + pair_sems(1) + pair_sems(groups)
    kernel = functools.partial(grads_kernel, groups)
    return call(kernel, number, shapes, scratch, (grad_pack, gains), "sum_grads")


def pair_permute(value):
    dp = lax.axis_size("dp")
    return lax.ppermute(value, "dp", [(i, i + 1 - 2 * (i % 2)) for i in range(dp)])


def line_permute(value, shift):
    dp = lax.axis_size("dp")
    groups = dp // 2
    perm = [(i, ((i // 2 + shift) % groups) * 2 + i % 2) for i in range(dp)]
    return lax.ppermute(value, "dp", perm)


def line_gather(value):
    groups = lax.axis_size("dp") // 2
    parts = [value] + [line_permute(value, groups - s) for s in range(1, groups)]
    both = jnp.stack(parts + parts)
    return lax.dynamic_slice_in_dim(both, groups - lax.axis_index("dp") // 2, groups, 0)


def pair_gather(value):
    other = pair_permute(value)
    side = lax.rem(lax.axis_index("dp"), 2)
    first = jnp.where(side == 0, value, other)
    second = jnp.where(side == 0, other, value)
    return jnp.stack([first, second], axis=1)


def pair_sum(pack):
    dp = lax.axis_size("dp")
    side = lax.rem(lax.axis_index("dp"), 2)
    pairs = pack.reshape(dp // 2, 2, *pack.shape[1:])
    own = lax.dynamic_index_in_dim(pairs, side, 1, keepdims=False)
    other = pair_permute(lax.dynamic_index_in_dim(pairs, 1 - side, 1, keepdims=False))
    return (own.astype(jnp.float32) + other.astype(jnp.float32)).astype(pack.dtype)


def line_sum(blocks):
    groups = lax.axis_size("dp") // 2
    group = lax.axis_index("dp") // 2
    total = None
    for s in range(groups):
        block = lax.dynamic_index_in_dim(blocks, lax.rem(group + s, groups), 0, keepdims=False)
        term = (line_permute(block, s) if s else block).astype(jnp.float32)
        total = term if total is None else total + term
    return total


def padded_rows(value):
    rows = value.shape[-2]
    extra = -rows % 16
    return jnp.pad(value, [(0, 0)] * (value.ndim - 2) + [(0, extra), (0, 0)])


def doc_positions(seg_ids):
    length_all = seg_ids.shape[-1]
    token_index = jnp.arange(length_all, dtype=jnp.int32)
    starts = jnp.concatenate(
        [token_index[..., :1] == 0, seg_ids[..., 1:] != seg_ids[..., :-1]], axis=-1
    )
    doc_start = lax.cummax(jnp.where(starts, token_index, 0), axis=seg_ids.ndim - 1)
    return token_index - doc_start


def rope_tables(positions):
    half_dim = HEAD_DIM // 2
    exponents = jnp.arange(half_dim, dtype=jnp.float32) * (2.0 / HEAD_DIM)
    inverse = jnp.exp(-math.log(rope_base) * exponents)
    angles = positions.astype(jnp.float32)[..., None] * inverse
    cosine = jnp.cos(angles)
    sine = jnp.sin(angles)
    return (jnp.concatenate([cosine, cosine], axis=-1), jnp.concatenate([sine, sine], axis=-1))


def rotate(values, cosine, sine):
    half_dim = values.shape[-1] // 2
    turned = jnp.concatenate([-values[..., half_dim:], values[..., :half_dim]], axis=-1)
    return values * cosine[..., None, :] + turned * sine[..., None, :]


def matmul_f32(left, right):
    return jnp.dot(left, right, preferred_element_type=jnp.float32)


def inner_rows(left, right):
    return lax.dot_general(
        left, right, (((0,), (0,)), ((), ())), preferred_element_type=jnp.float32
    )


def inner_cols(left, right):
    return lax.dot_general(
        left, right, (((1,), (1,)), ((), ())), preferred_element_type=jnp.float32
    )


def norm_in(residual, gain):
    rows_f32 = residual.astype(jnp.bfloat16).astype(jnp.float32)
    row_scale = lax.rsqrt(jnp.mean(rows_f32 * rows_f32, axis=1, keepdims=True) + norm_eps)
    normed = (rows_f32 * row_scale * gain.astype(jnp.float32)).astype(jnp.bfloat16)
    return (rows_f32, row_scale, normed)


def summed(pieces):
    return jnp.sum(pieces.astype(jnp.float32), axis=0)


def columns_over(gathered):
    peers, rows, width = gathered.shape
    return jnp.moveaxis(gathered, 0, 1).reshape(rows, peers * width)


def norm_back(grad_normed, rows_f32, row_scale, gain):
    width = rows_f32.shape[1]
    gain_f32 = gain.astype(jnp.float32)
    cubed = row_scale * row_scale * row_scale
    inner = jnp.sum(grad_normed * gain_f32 * rows_f32, axis=1, keepdims=True)
    resid_grad = gain_f32 * row_scale * grad_normed - rows_f32 * cubed * inner / width
    gain_term = jnp.sum(grad_normed * rows_f32 * row_scale, axis=0)
    return (resid_grad, gain_term)


def head_views(query_turned, keys_all, values_all):
    own_rows = query_turned.shape[0]
    group_size = HEADS // KV_HEADS
    query_heads = query_turned.reshape(own_rows, KV_HEADS, group_size, HEAD_DIM)
    key_heads = keys_all.reshape(keys_all.shape[0], KV_HEADS, HEAD_DIM)
    value_heads = values_all.reshape(values_all.shape[0], KV_HEADS, HEAD_DIM)
    return (query_heads, key_heads, value_heads)


def masked_logits(query_heads, key_heads, allowed):
    scores = jnp.einsum(
        "qkgd,tkd->kgqt", query_heads, key_heads, preferred_element_type=jnp.float32
    )
    return jnp.where(allowed, scores * (1.0 / math.sqrt(HEAD_DIM)), masked_value)


def attend(query_turned, keys_all, values_all, allowed):
    query_heads, key_heads, value_heads = head_views(query_turned, keys_all, values_all)
    logits = masked_logits(query_heads, key_heads, allowed)
    row_max = jnp.max(logits, axis=3, keepdims=True)
    raised = jnp.exp(logits - row_max)
    row_total = jnp.sum(raised, axis=3, keepdims=True)
    weights_low = (raised / row_total).astype(jnp.bfloat16)
    mixed = jnp.einsum(
        "kgqt,tkd->qkgd", weights_low, value_heads, preferred_element_type=jnp.float32
    )
    return (mixed.reshape(query_turned.shape[0], -1), row_max + jnp.log(row_total))


def attend_back(query_turned, keys_all, values_all, allowed, log_total, grad_mixed):
    query_heads, key_heads, value_heads = head_views(query_turned, keys_all, values_all)
    logits = masked_logits(query_heads, key_heads, allowed)
    weights = jnp.exp(logits - log_total)
    grad_heads = grad_mixed.reshape(query_heads.shape)
    grad_weights = jnp.einsum(
        "qkgd,tkd->kgqt", grad_heads, value_heads, preferred_element_type=jnp.float32
    )
    delta = jnp.sum(weights * grad_weights, axis=3, keepdims=True)
    grad_scores = (weights * (grad_weights - delta) * (1.0 / math.sqrt(HEAD_DIM))).astype(
        jnp.bfloat16
    )
    grad_query = jnp.einsum(
        "kgqt,tkd->qkgd", grad_scores, key_heads, preferred_element_type=jnp.float32
    )
    grad_keys = jnp.einsum(
        "kgqt,qkgd->tkd", grad_scores, query_heads, preferred_element_type=jnp.float32
    )
    grad_values = jnp.einsum(
        "kgqt,qkgd->tkd",
        weights.astype(jnp.bfloat16),
        grad_heads,
        preferred_element_type=jnp.float32,
    )
    row_count = keys_all.shape[0]
    return (
        grad_query.reshape(query_turned.shape[0], -1),
        grad_keys.reshape(row_count, -1),
        grad_values.reshape(row_count, -1),
    )


def on_device(
    block_input,
    segments,
    attend_gain,
    query_weight,
    key_weight,
    value_weight,
    mix_weight,
    feed_gain,
    gate_weight,
    up_weight,
    down_weight,
    cotangent,
):
    bf16, f32 = jnp.bfloat16, jnp.float32
    width = block_input.shape[1] // 2
    own_rows = block_input.shape[0] * 2
    mp = lax.axis_size("mp")
    dp = lax.axis_size("dp")
    row_count = own_rows * mp
    first_row = lax.axis_index("mp") * own_rows
    qw, kw, ff = query_weight.shape[2], key_weight.shape[2], gate_weight.shape[2]
    depth = query_weight.shape[1]
    aw = 2 * qw + 2 * kw
    packed = jnp.concatenate(
        [
            query_weight,
            key_weight,
            value_weight,
            jnp.swapaxes(mix_weight, 1, 2),
            gate_weight,
            up_weight,
            jnp.swapaxes(down_weight, 1, 2),
        ],
        axis=2,
    )
    total_width = packed.shape[2]
    residual = block_input.reshape(own_rows, width).astype(f32)
    rows_f32, row_scale, normed = norm_in(residual, attend_gain[0])
    normed_all, attend_all, feed_first = gather_weights(
        0, normed, packed[:, :, :aw].reshape(LAYERS * depth, aw), padded_rows(packed[0, :, aw:])
    )
    attend_all = jnp.moveaxis(attend_all.reshape(mp, dp, LAYERS, depth, aw), 2, 1)
    attend_all = attend_all.reshape(mp, LAYERS, width, aw)
    feed_all = [feed_first[:, :depth].reshape(width, total_width - aw)] + [None] * (LAYERS - 1)
    normed_all, *feed_own = lax.optimization_barrier(
        (normed_all, *[packed[i, :, aw:] for i in range(1, LAYERS)])
    )
    feed_line = [line_gather(part) for part in feed_own]
    attend_full, feed_full = ([], [])
    for layer in range(LAYERS):
        part = attend_all[:, layer]
        attend_full.append(
            (
                columns_over(part[:, :, :qw]),
                columns_over(part[:, :, qw : qw + kw]),
                columns_over(part[:, :, qw + kw : qw + 2 * kw]),
                columns_over(part[:, :, qw + 2 * kw :]),
            )
        )

    seg_ids = segments[0]
    positions = doc_positions(seg_ids)
    my_segs = lax.dynamic_slice_in_dim(seg_ids, first_row, own_rows, 0)
    cos_all, sin_all = rope_tables(positions)
    cosine = lax.dynamic_slice_in_dim(cos_all, first_row, own_rows, 0)
    sine = lax.dynamic_slice_in_dim(sin_all, first_row, own_rows, 0)
    key_index = jnp.arange(row_count, dtype=jnp.int32)
    query_index = first_row + jnp.arange(own_rows, dtype=jnp.int32)
    allowed = (key_index[None, :] <= query_index[:, None]) & (seg_ids[None, :] == my_segs[:, None])

    attend_saved = []
    feed_saved = []
    for layer in range(LAYERS):
        query_full, key_full, value_full, mix_turned = attend_full[layer]
        if layer > 0:
            rows_f32, row_scale, normed = norm_in(residual, attend_gain[layer])
            if layer == 1:
                normed, *feed_line = lax.optimization_barrier((normed, *feed_line))
                for i, other in enumerate(feed_line):
                    feed_all[i + 1] = other.reshape(width, total_width - aw)
            (normed_all,) = exchange(10 + layer, [normed])
        normed_all = normed_all.reshape(row_count, width)
        query_rows = matmul_f32(normed, query_full).astype(bf16).astype(f32)
        key_rows = matmul_f32(normed_all, key_full).astype(bf16).astype(f32)
        values_all = matmul_f32(normed_all, value_full).astype(bf16)
        query_turned = rotate(query_rows.reshape(own_rows, HEADS, HEAD_DIM), cosine, sine)
        query_turned = query_turned.reshape(own_rows, -1).astype(bf16)
        keys_all = rotate(key_rows.reshape(row_count, KV_HEADS, HEAD_DIM), cos_all, sin_all)
        keys_all = keys_all.reshape(row_count, -1).astype(bf16)
        mixed, log_total = attend(query_turned, keys_all, values_all, allowed)
        mixed = mixed.astype(bf16)
        residual = residual + inner_cols(mixed, mix_turned)
        attend_saved.append(
            (
                rows_f32,
                row_scale,
                normed_all,
                query_turned,
                keys_all,
                values_all,
                log_total,
                mixed,
            )
        )
        rows_two, scale_two, normed_two = norm_in(residual, feed_gain[layer])
        if layer == 0:
            normed_two, *feed_line = lax.optimization_barrier((normed_two, *feed_line))
            for i, part in enumerate(feed_line):
                feed_line[i] = pair_gather(part)
        feed = feed_all[layer]
        feed_full.append((feed[:, :ff], feed[:, ff : 2 * ff], feed[:, 2 * ff :]))
        (normed_two,) = exchange(20 + layer, [normed_two])
        normed_two = normed_two.reshape(row_count, width)
        gate_full, up_full, down_turned = feed_full[layer]
        gate_out = matmul_f32(normed_two, gate_full)
        up_out = matmul_f32(normed_two, up_full)
        hidden = (jax.nn.silu(gate_out) * up_out).astype(bf16)
        part = inner_cols(hidden, down_turned).astype(bf16).reshape(mp, own_rows, width)
        (part,) = exchange(30 + layer, (), (), [part])
        residual = residual + part
        feed_saved.append((rows_two, scale_two, normed_two, gate_out, up_out, hidden))
    block_output = residual.astype(bf16).reshape(own_rows // 2, 2 * width)

    grad_resid = cotangent.reshape(own_rows, width).astype(f32)
    attend_terms = [None] * LAYERS
    feed_terms = [None] * LAYERS
    grads = [None] * LAYERS
    feed_grads = [None] * LAYERS

    def attend_grads(layer, received):
        grad_all, mixed_cols, dqkv_cols = [a.reshape(row_count, -1) for a in received]
        normed_all = attend_saved[layer][2]
        return jnp.concatenate(
            [inner_rows(normed_all, dqkv_cols), inner_rows(grad_all, mixed_cols)], axis=1
        )

    late = None
    for layer in range(LAYERS - 1, -1, -1):
        rows_two, scale_two, normed_two, gate_out, up_out, hidden = feed_saved[layer]
        gate_full, up_full, down_turned = feed_full[layer]
        got = exchange(
            40 + layer,
            [grad_resid.astype(bf16)] + ([late[0]] if late else []),
            late[1:] if late else [],
        )
        grad_full = got[0].reshape(row_count, width)
        if late:
            pack = jnp.concatenate(
                [attend_grads(layer + 1, got[1:]), feed_grads[layer + 1]], axis=1
            ).astype(bf16)
            pairs = pair_sum(pack.reshape(dp, depth, total_width))
        grad_hidden = matmul_f32(grad_full, down_turned)
        down_term = inner_rows(grad_full, hidden)
        sigmoid_gate = jax.nn.sigmoid(gate_out)
        grad_gate = (
            grad_hidden * up_out * sigmoid_gate * (1.0 + gate_out * (1.0 - sigmoid_gate))
        ).astype(bf16)
        grad_up = (grad_hidden * gate_out * sigmoid_gate).astype(bf16)
        grad_normed = (inner_cols(grad_gate, gate_full) + inner_cols(grad_up, up_full)).astype(bf16)
        (part,) = exchange(50 + layer, (), (), [grad_normed.reshape(mp, own_rows, width)])
        feed_grads[layer] = jnp.concatenate(
            [inner_rows(normed_two, grad_gate), inner_rows(normed_two, grad_up), down_term], axis=1
        )
        resid_grad, feed_terms[layer] = norm_back(
            part, rows_two, scale_two, feed_gain[layer]
        )
        grad_resid = grad_resid + resid_grad
        (
            rows_f32,
            row_scale,
            normed_all,
            query_turned,
            keys_all,
            values_all,
            log_total,
            mixed,
        ) = attend_saved[layer]
        query_full, key_full, value_full, mix_turned = attend_full[layer]
        grad_low = grad_resid.astype(bf16)
        grad_mixed = matmul_f32(grad_low, mix_turned).astype(bf16)
        grad_query, grad_keys, grad_values = attend_back(
            query_turned, keys_all, values_all, allowed, log_total, grad_mixed
        )
        key_value = jnp.concatenate([grad_keys, grad_values], axis=1).astype(bf16)
        if late:
            key_value, pairs = lax.optimization_barrier((key_value, pairs))
            grads[layer + 1] = line_sum(pairs)
        (key_value,) = exchange(
            60 + layer, (), (), [key_value.reshape(mp, own_rows, 2 * mp * kw)]
        )
        query_back = rotate(grad_query.reshape(own_rows, HEADS, HEAD_DIM), cosine, -sine)
        query_back = query_back.reshape(own_rows, -1).astype(bf16)
        key_back = rotate(
            key_value[:, : mp * kw].reshape(own_rows, KV_HEADS, HEAD_DIM), cosine, -sine
        )
        key_back = key_back.reshape(own_rows, -1).astype(bf16)
        value_back = key_value[:, mp * kw :].astype(bf16)
        grad_normed = (
            inner_cols(query_back, query_full)
            + inner_cols(key_back, key_full)
            + inner_cols(value_back, value_full)
        )
        resid_grad, attend_terms[layer] = norm_back(
            grad_normed, rows_f32, row_scale, attend_gain[layer]
        )
        grad_resid = grad_resid + resid_grad
        dqkv = jnp.concatenate(
            [a.reshape(own_rows, mp, -1) for a in (query_back, key_back, value_back)], axis=2
        )
        late = (
            grad_low,
            jnp.moveaxis(mixed.reshape(own_rows, mp, qw), 1, 0),
            jnp.moveaxis(dqkv, 1, 0),
        )
    gains = jnp.concatenate([jnp.stack(attend_terms), jnp.stack(feed_terms)], axis=0)
    gains = jnp.concatenate([gains, jnp.zeros((16 - 2 * LAYERS, width), f32)], axis=0)
    gains, *sent = lax.optimization_barrier((gains, *grads[1:]))
    grads[1:] = sent
    got = exchange(2, [late[0], gains], late[1:])
    gains = summed(got[1])
    pack = jnp.concatenate(
        [attend_grads(0, (got[0], got[2], got[3])), feed_grads[0]], axis=1
    ).astype(bf16)
    total, gains = sum_grads(3, padded_rows(pack.reshape(dp, depth, total_width)), gains)
    grads[0] = total[:depth]
    total = jnp.stack(grads)
    input_grad = grad_resid.reshape(own_rows // 2, 2 * width)
    return (
        block_output,
        input_grad,
        gains[:LAYERS],
        total[:, :, :qw],
        total[:, :, qw : qw + kw],
        total[:, :, qw + kw : qw + 2 * kw],
        jnp.swapaxes(total[:, :, qw + 2 * kw : aw], 1, 2),
        gains[LAYERS : 2 * LAYERS],
        total[:, :, aw : aw + ff],
        total[:, :, aw + ff : aw + 2 * ff],
        jnp.swapaxes(total[:, :, aw + 2 * ff :], 1, 2),
    )


def solution(mesh):
    in_specs = (
        P(("dp", "mp"), None),
        P("dp", None),
        P(),
        P(None, "dp", "mp"),
        P(None, "dp", "mp"),
        P(None, "dp", "mp"),
        P(None, "mp", "dp"),
        P(),
        P(None, "dp", "mp"),
        P(None, "dp", "mp"),
        P(None, "mp", "dp"),
        P(("dp", "mp"), None),
    )
    out_specs = (
        P(("dp", "mp"), None),
        P(("dp", "mp"), None),
        P(),
        P(None, "dp", "mp"),
        P(None, "dp", "mp"),
        P(None, "dp", "mp"),
        P(None, "mp", "dp"),
        P(),
        P(None, "dp", "mp"),
        P(None, "dp", "mp"),
        P(None, "mp", "dp"),
    )
    return jax.shard_map(
        on_device, mesh=mesh, in_specs=in_specs, out_specs=out_specs, check_vma=False
    )
```

```python
import functools
import math

import jax
import jax.numpy as jnp
from jax import lax
from jax.experimental import pallas as pl
from jax.experimental.pallas import tpu as pltpu
from jax.sharding import PartitionSpec as P

HEADS = 9
KV_HEADS = 3
HEAD_DIM = 64
LAYERS = 2


norm_eps = 1e-05
rope_base = 100000.0
masked_value = -1e30


MESH = pl.DeviceIdType.MESH


def greet(devices):
    barrier = pltpu.get_barrier_semaphore()
    for device in devices:
        pl.semaphore_signal(barrier, inc=1, device_id=device, device_id_type=MESH)
    pl.semaphore_wait(barrier, len(devices))


def send(source, target, sems, at, device):
    copy = pltpu.make_async_remote_copy(
        src_ref=source,
        dst_ref=target,
        send_sem=sems[0].at[at],
        recv_sem=sems[1].at[at],
        device_id=device,
        device_id_type=MESH,
    )
    copy.start()
    return copy


def pair_sems(count):
    return [pltpu.SemaphoreType.DMA((count,)), pltpu.SemaphoreType.DMA((count,))]


def call(kernel, number, shapes, scratch, args, name):
    space = pl.BlockSpec(memory_space=pltpu.VMEM)
    return pl.pallas_call(
        kernel,
        out_shape=shapes,
        in_specs=[space] * len(args),
        out_specs=[space] * len(shapes),
        scratch_shapes=scratch,
        compiler_params=pltpu.CompilerParams(
            collective_id=number, has_side_effects=True, vmem_limit_bytes=48 * 1024 * 1024
        ),
        name=name,
    )(*args)


CHUNKS = 2


def model_kernel(n_whole, n_split, n_sum, peers, *refs):
    n_in = n_whole + n_split + n_sum
    ins, refs = refs[:n_in], refs[n_in:]
    outs, refs = refs[:n_in], refs[n_in:]
    from_core, refs = refs[:n_sum], refs[n_sum:]
    for_far, refs = refs[:n_sum], refs[n_sum:]
    from_far, refs = refs[:n_sum], refs[n_sum:]
    whole_near, whole_far, whole_pass = refs[0:2], refs[2:4], refs[4:6]
    split_sems, sum_near, sum_mid, sum_far = refs[6:8], refs[8:10], refs[10:12], refs[12:14]
    local_sem = refs[14]
    me = lax.axis_index("mp")
    chip, core = me // 2, lax.rem(me, 2)
    near = chip * 2 + (1 - core)
    far = (1 - chip) * 2 + core
    cross = (1 - chip) * 2 + (1 - core)
    others = [near, far, cross]
    greet([{"mp": o} for o in (others if n_split else others[:2])])
    ready, waits = ([], [])
    first_sum = n_whole + n_split
    mids = []
    for i in range(n_sum):
        rows = outs[first_sum + i].shape[0] // CHUNKS
        for k in range(CHUNKS):
            cut = pl.ds(k * rows, rows)
            at = i * CHUNKS + k
            mids.append(
                send(
                    ins[first_sum + i].at[cross, cut],
                    from_core[i].at[0, cut],
                    sum_mid,
                    at,
                    {"mp": near},
                )
            )
        ready.append(
            send(ins[first_sum + i].at[near], from_core[i].at[1], sum_near, i, {"mp": near})
        )
    passes = []
    for i in range(n_whole):
        rows = ins[i].shape[0] // CHUNKS
        for k in range(CHUNKS):
            cut = pl.ds(k * rows, rows)
            at = i * CHUNKS + k
            passes.append(
                send(ins[i].at[cut], outs[i].at[me, cut], whole_far, at, {"mp": far})
            )
        waits.append(send(ins[i], outs[i].at[me], whole_near, i, {"mp": near}))
        local = pltpu.make_async_copy(ins[i], outs[i].at[me], local_sem.at[i])
        local.start()
        waits.append(local)
    for j in range(n_split):
        i = n_whole + j
        for s, o in enumerate(others):
            waits.append(
                send(ins[i].at[o], outs[i].at[me], split_sems, j * 3 + s, {"mp": o})
            )
        local = pltpu.make_async_copy(ins[i].at[me], outs[i].at[me], local_sem.at[i])
        local.start()
        waits.append(local)
    fars = []
    for i in range(n_sum):
        rows = outs[first_sum + i].shape[0] // CHUNKS
        for k in range(CHUNKS):
            cut = pl.ds(k * rows, rows)
            at = i * CHUNKS + k
            mids[at].wait()
            for_far[i][cut] = (
                ins[first_sum + i][far, cut].astype(jnp.float32)
                + from_core[i][0, cut].astype(jnp.float32)
            ).astype(for_far[i].dtype)
            fars.append(
                send(for_far[i].at[cut], from_far[i].at[cut], sum_far, at, {"mp": far})
            )
    for i in range(n_whole):
        rows = ins[i].shape[0] // CHUNKS
        for k in range(CHUNKS):
            cut = pl.ds(k * rows, rows)
            at = i * CHUNKS + k
            passes[at].wait()
            waits.append(
                send(outs[i].at[far, cut], outs[i].at[far, cut], whole_pass, at, {"mp": near})
            )
    for i in range(n_sum):
        ready[i].wait()
        for k in range(CHUNKS):
            fars[i * CHUNKS + k].wait()
        outs[first_sum + i][...] = (
            ins[first_sum + i][me].astype(jnp.float32)
            + from_core[i][1].astype(jnp.float32)
            + from_far[i][...].astype(jnp.float32)
        )
    for copy in waits:
        copy.wait()


def exchange(number, whole=(), split=(), sums=()):
    peers = lax.axis_size("mp")
    args = [*whole, *split, *sums]
    shapes = [jax.ShapeDtypeStruct((peers, *a.shape), a.dtype) for a in whole]
    shapes += [jax.ShapeDtypeStruct(a.shape, a.dtype) for a in split]
    shapes += [jax.ShapeDtypeStruct(a.shape[1:], jnp.float32) for a in sums]
    scratch = [pltpu.VMEM((2, *a.shape[1:]), a.dtype) for a in sums]
    scratch += [pltpu.VMEM(a.shape[1:], a.dtype) for a in sums] * 2
    n_whole, n_split, n_sum = max(1, len(whole)), max(1, len(split)), max(1, len(sums))
    scratch += pair_sems(n_whole) + pair_sems(n_whole * CHUNKS) + pair_sems(n_whole * CHUNKS)
    scratch += pair_sems(n_split * 3) + pair_sems(n_sum)
    scratch += pair_sems(n_sum * CHUNKS) + pair_sems(n_sum * CHUNKS)
    scratch += [pltpu.SemaphoreType.DMA((n_whole + n_split,))]
    kernel = functools.partial(model_kernel, len(whole), len(split), len(sums), peers)
    return call(kernel, number, shapes, scratch, args, "model_exchange")


def weights_kernel(
    groups,
    rows_ref,
    attend_ref,
    feed_ref,
    rows_out,
    attend_out,
    feed_out,
    zf0,
    zf1,
    za0,
    za1,
    xf0,
    xf1,
    xa0,
    xa1,
    y0,
    y1,
    c0,
    c1,
    n0,
    n1,
    local_sem,
):
    zf, za, xf, xa, ys, cs, ns = (
        (zf0, zf1), (za0, za1), (xf0, xf1), (xa0, xa1), (y0, y1), (c0, c1), (n0, n1)
    )
    me, index = lax.axis_index("mp"), lax.axis_index("dp")
    chip, core = me // 2, lax.rem(me, 2)
    near = {"mp": chip * 2 + (1 - core)}
    far_index = (1 - chip) * 2 + core
    far = {"mp": far_index}
    group, side = index // 2, lax.rem(index, 2)
    beside = {"dp": group * 2 + (1 - side)}
    line = [{"dp": lax.rem(group + s, groups) * 2 + side} for s in range(1, groups)]
    greet([near, far, beside, *line])
    waits = []
    to_line, to_beside, to_far = ([], [], [])
    n_far = send(rows_ref, rows_out.at[me], ns, 0, far)
    waits.append(send(rows_ref, rows_out.at[me], ns, 1, near))

    def along(s):
        to_line.append(
            (
                send(attend_ref, attend_out.at[me, index], za, s, line[s - 1]),
                send(feed_ref, feed_out.at[index], zf, s, line[s - 1]),
            )
        )

    along(1)
    to_beside.append(send(attend_ref, attend_out.at[me, index], xa, 0, beside))
    waits.append(send(feed_ref, feed_out.at[index], xf, 0, beside))
    to_far.append((index, send(attend_ref, attend_out.at[me, index], ys, 0, far)))
    waits.append(send(attend_ref, attend_out.at[me, index], cs, 0, near))
    for i, (a, o) in enumerate(
        (
            (rows_ref, rows_out.at[me]),
            (attend_ref, attend_out.at[me, index]),
            (feed_ref, feed_out.at[index]),
        )
    ):
        local = pltpu.make_async_copy(a, o, local_sem.at[i])
        local.start()
        waits.append(local)
    n_far.wait()
    waits.append(send(rows_out.at[far_index], rows_out.at[far_index], ns, 2, near))

    def share(at, block):
        to_far.append(
            (block, send(attend_out.at[me, block], attend_out.at[me, block], ys, at, far))
        )
        waits.append(send(attend_out.at[me, block], attend_out.at[me, block], cs, at, near))

    def pass_on(at):
        block, copy = to_far[at]
        copy.wait()
        waits.append(
            send(
                attend_out.at[far_index, block],
                attend_out.at[far_index, block],
                cs,
                2 * groups + at,
                near,
            )
        )

    for s in range(1, groups):
        block = lax.rem(group + groups - s, groups) * 2 + side
        to_line[s - 1][0].wait()
        to_beside.append(
            send(attend_out.at[me, block], attend_out.at[me, block], xa, s, beside)
        )
        share(s, block)
        to_line[s - 1][1].wait()
        if s < groups - 1:
            along(s + 1)
        waits.append(send(feed_out.at[block], feed_out.at[block], xf, s, beside))
        pass_on(s - 1)
    for s in range(groups):
        block = lax.rem(group + groups - s, groups) * 2 + (1 - side)
        to_beside[s].wait()
        share(groups + s, block)
        pass_on(groups - 1 + s)
    pass_on(2 * groups - 1)
    for copy in waits:
        copy.wait()


def gather_weights(number, rows, attend, feed):
    mp, dp = lax.axis_size("mp"), lax.axis_size("dp")
    groups = dp // 2
    shapes = [
        jax.ShapeDtypeStruct((mp, *rows.shape), rows.dtype),
        jax.ShapeDtypeStruct((mp, dp, *attend.shape), attend.dtype),
        jax.ShapeDtypeStruct((dp, *feed.shape), feed.dtype),
    ]
    scratch = pair_sems(groups) * 4 + pair_sems(2 * groups) + pair_sems(4 * groups) + pair_sems(3)
    scratch += [pltpu.SemaphoreType.DMA((3,))]
    kernel = functools.partial(weights_kernel, groups)
    return call(kernel, number, shapes, scratch, (rows, attend, feed), "gather_weights")


def grads_kernel(
    groups,
    grad_ref,
    gain_ref,
    grad_out,
    gain_out,
    x_in,
    z_send,
    z_in,
    gain_x,
    gain_send,
    gain_z,
    x0,
    x1,
    z0,
    z1,
    gx0,
    gx1,
    gz0,
    gz1,
):
    xs, zs, gx, gz = (x0, x1), (z0, z1), (gx0, gx1), (gz0, gz1)
    index = lax.axis_index("dp")
    group, side = index // 2, lax.rem(index, 2)
    beside = {"dp": group * 2 + (1 - side)}
    line = [lax.rem(group + s, groups) for s in range(groups)]
    greet([beside] + [{"dp": g * 2 + side} for g in line[1:]])
    order = [*range(1, groups), 0]
    gain_copy = send(gain_ref, gain_x, gx, 0, beside)

    def cross(s):
        return send(grad_ref.at[line[s] * 2 + (1 - side)], x_in.at[s], xs, s, beside)

    copy = cross(order[0])
    gain_copy.wait()
    gain_send[...] = gain_ref[...] + gain_x[...]
    later = []
    for s in range(1, groups):
        device = {"dp": line[s] * 2 + side}
        gain_copy = send(gain_send, gain_z.at[s], gz, s, device)
        copy.wait()
        copy = cross(order[s])
        z_send[s] = (
            grad_ref[line[s] * 2 + side].astype(jnp.float32) + x_in[s].astype(jnp.float32)
        ).astype(z_send.dtype)
        later.append((send(z_send.at[s], z_in.at[s], zs, s, device), gain_copy))
    copy.wait()
    grad_out[...] = grad_ref[index].astype(jnp.float32) + x_in[0].astype(jnp.float32)
    gain_out[...] = gain_send[...]
    for s in range(1, groups):
        later[s - 1][1].wait()
        gain_out[...] += gain_z[s]
        later[s - 1][0].wait()
        grad_out[...] += z_in[s].astype(jnp.float32)


def sum_grads(number, grad_pack, gains):
    dp = lax.axis_size("dp")
    groups = dp // 2
    block = grad_pack.shape[1:]
    shapes = [
        jax.ShapeDtypeStruct(block, jnp.float32),
        jax.ShapeDtypeStruct(gains.shape, jnp.float32),
    ]
    scratch = [pltpu.VMEM((groups, *block), grad_pack.dtype)] * 3
    scratch += [pltpu.VMEM(gains.shape, jnp.float32)] * 2
    scratch += [pltpu.VMEM((groups, *gains.shape), jnp.float32)]
    scratch += pair_sems(groups) * 2 + pair_sems(1) + pair_sems(groups)
    kernel = functools.partial(grads_kernel, groups)
    return call(kernel, number, shapes, scratch, (grad_pack, gains), "sum_grads")


def doc_positions(seg_ids):
    length_all = seg_ids.shape[-1]
    token_index = jnp.arange(length_all, dtype=jnp.int32)
    starts = jnp.concatenate(
        [token_index[..., :1] == 0, seg_ids[..., 1:] != seg_ids[..., :-1]], axis=-1
    )
    doc_start = lax.cummax(jnp.where(starts, token_index, 0), axis=seg_ids.ndim - 1)
    return token_index - doc_start


def rope_tables(positions):
    half_dim = HEAD_DIM // 2
    exponents = jnp.arange(half_dim, dtype=jnp.float32) * (2.0 / HEAD_DIM)
    inverse = jnp.exp(-math.log(rope_base) * exponents)
    angles = positions.astype(jnp.float32)[..., None] * inverse
    cosine = jnp.cos(angles)
    sine = jnp.sin(angles)
    return (jnp.concatenate([cosine, cosine], axis=-1), jnp.concatenate([sine, sine], axis=-1))


def rotate(values, cosine, sine):
    half_dim = values.shape[-1] // 2
    turned = jnp.concatenate([-values[..., half_dim:], values[..., :half_dim]], axis=-1)
    return values * cosine[..., None, :] + turned * sine[..., None, :]


def matmul_f32(left, right):
    return jnp.dot(left, right, preferred_element_type=jnp.float32)


def inner_rows(left, right):
    return lax.dot_general(
        left, right, (((0,), (0,)), ((), ())), preferred_element_type=jnp.float32
    )


def inner_cols(left, right):
    return lax.dot_general(
        left, right, (((1,), (1,)), ((), ())), preferred_element_type=jnp.float32
    )


def norm_in(residual, gain):
    rows_f32 = residual.astype(jnp.bfloat16).astype(jnp.float32)
    row_scale = lax.rsqrt(jnp.mean(rows_f32 * rows_f32, axis=1, keepdims=True) + norm_eps)
    normed = (rows_f32 * row_scale * gain.astype(jnp.float32)).astype(jnp.bfloat16)
    return (rows_f32, row_scale, normed)


def summed(pieces):
    return jnp.sum(pieces.astype(jnp.float32), axis=0)


def columns_over(gathered):
    peers, rows, width = gathered.shape
    return jnp.moveaxis(gathered, 0, 1).reshape(rows, peers * width)


def norm_back(grad_normed, rows_f32, row_scale, gain):
    width = rows_f32.shape[1]
    gain_f32 = gain.astype(jnp.float32)
    cubed = row_scale * row_scale * row_scale
    inner = jnp.sum(grad_normed * gain_f32 * rows_f32, axis=1, keepdims=True)
    resid_grad = gain_f32 * row_scale * grad_normed - rows_f32 * cubed * inner / width
    gain_term = jnp.sum(grad_normed * rows_f32 * row_scale, axis=0)
    return (resid_grad, gain_term)


def head_views(query_turned, keys_all, values_all):
    own_rows = query_turned.shape[0]
    group_size = HEADS // KV_HEADS
    query_heads = query_turned.reshape(own_rows, KV_HEADS, group_size, HEAD_DIM)
    key_heads = keys_all.reshape(keys_all.shape[0], KV_HEADS, HEAD_DIM)
    value_heads = values_all.reshape(values_all.shape[0], KV_HEADS, HEAD_DIM)
    return (query_heads, key_heads, value_heads)


def masked_logits(query_heads, key_heads, allowed):
    scores = jnp.einsum(
        "qkgd,tkd->kgqt", query_heads, key_heads, preferred_element_type=jnp.float32
    )
    return jnp.where(allowed, scores * (1.0 / math.sqrt(HEAD_DIM)), masked_value)


def attend(query_turned, keys_all, values_all, allowed):
    query_heads, key_heads, value_heads = head_views(query_turned, keys_all, values_all)
    logits = masked_logits(query_heads, key_heads, allowed)
    row_max = jnp.max(logits, axis=3, keepdims=True)
    raised = jnp.exp(logits - row_max)
    row_total = jnp.sum(raised, axis=3, keepdims=True)
    weights_low = (raised / row_total).astype(jnp.bfloat16)
    mixed = jnp.einsum(
        "kgqt,tkd->qkgd", weights_low, value_heads, preferred_element_type=jnp.float32
    )
    return (mixed.reshape(query_turned.shape[0], -1), row_max + jnp.log(row_total))


def attend_back(query_turned, keys_all, values_all, allowed, log_total, grad_mixed):
    query_heads, key_heads, value_heads = head_views(query_turned, keys_all, values_all)
    logits = masked_logits(query_heads, key_heads, allowed)
    weights = jnp.exp(logits - log_total)
    grad_heads = grad_mixed.reshape(query_heads.shape)
    grad_weights = jnp.einsum(
        "qkgd,tkd->kgqt", grad_heads, value_heads, preferred_element_type=jnp.float32
    )
    delta = jnp.sum(weights * grad_weights, axis=3, keepdims=True)
    grad_scores = (weights * (grad_weights - delta) * (1.0 / math.sqrt(HEAD_DIM))).astype(
        jnp.bfloat16
    )
    grad_query = jnp.einsum(
        "kgqt,tkd->qkgd", grad_scores, key_heads, preferred_element_type=jnp.float32
    )
    grad_keys = jnp.einsum(
        "kgqt,qkgd->tkd", grad_scores, query_heads, preferred_element_type=jnp.float32
    )
    grad_values = jnp.einsum(
        "kgqt,qkgd->tkd",
        weights.astype(jnp.bfloat16),
        grad_heads,
        preferred_element_type=jnp.float32,
    )
    row_count = keys_all.shape[0]
    return (
        grad_query.reshape(query_turned.shape[0], -1),
        grad_keys.reshape(row_count, -1),
        grad_values.reshape(row_count, -1),
    )


def on_device(
    block_input,
    segments,
    attend_gain,
    query_weight,
    key_weight,
    value_weight,
    mix_weight,
    feed_gain,
    gate_weight,
    up_weight,
    down_weight,
    cotangent,
):
    bf16, f32 = jnp.bfloat16, jnp.float32
    width = block_input.shape[1] // 2
    own_rows = block_input.shape[0] * 2
    mp = lax.axis_size("mp")
    dp = lax.axis_size("dp")
    row_count = own_rows * mp
    first_row = lax.axis_index("mp") * own_rows
    qw, kw, ff = query_weight.shape[2], key_weight.shape[2], gate_weight.shape[2]
    depth = query_weight.shape[1]
    aw = 2 * qw + 2 * kw
    packed = jnp.concatenate(
        [
            query_weight,
            key_weight,
            value_weight,
            jnp.swapaxes(mix_weight, 1, 2),
            gate_weight,
            up_weight,
            jnp.swapaxes(down_weight, 1, 2),
        ],
        axis=2,
    )
    total_width = packed.shape[2]
    packed = packed.reshape(LAYERS * depth, total_width)
    residual = block_input.reshape(own_rows, width).astype(f32)
    rows_f32, row_scale, normed = norm_in(residual, attend_gain[0])
    normed_all, attend_all, feed_all = gather_weights(0, normed, packed[:, :aw], packed[:, aw:])
    attend_all = jnp.moveaxis(attend_all.reshape(mp, dp, LAYERS, depth, aw), 2, 1)
    attend_all = attend_all.reshape(mp, LAYERS, width, aw)
    feed_all = jnp.moveaxis(feed_all.reshape(dp, LAYERS, depth, total_width - aw), 1, 0)
    feed_all = feed_all.reshape(LAYERS, width, total_width - aw)
    attend_full, feed_full = ([], [])
    for layer in range(LAYERS):
        part = attend_all[:, layer]
        attend_full.append(
            (
                columns_over(part[:, :, :qw]),
                columns_over(part[:, :, qw : qw + kw]),
                columns_over(part[:, :, qw + kw : qw + 2 * kw]),
                columns_over(part[:, :, qw + 2 * kw :]),
            )
        )
        feed = feed_all[layer]
        feed_full.append((feed[:, :ff], feed[:, ff : 2 * ff], feed[:, 2 * ff :]))

    seg_ids = segments[0]
    positions = doc_positions(seg_ids)
    my_segs = lax.dynamic_slice_in_dim(seg_ids, first_row, own_rows, 0)
    cos_all, sin_all = rope_tables(positions)
    cosine = lax.dynamic_slice_in_dim(cos_all, first_row, own_rows, 0)
    sine = lax.dynamic_slice_in_dim(sin_all, first_row, own_rows, 0)
    key_index = jnp.arange(row_count, dtype=jnp.int32)
    query_index = first_row + jnp.arange(own_rows, dtype=jnp.int32)
    allowed = (key_index[None, :] <= query_index[:, None]) & (seg_ids[None, :] == my_segs[:, None])

    attend_saved = []
    feed_saved = []
    for layer in range(LAYERS):
        query_full, key_full, value_full, mix_turned = attend_full[layer]
        if layer > 0:
            rows_f32, row_scale, normed = norm_in(residual, attend_gain[layer])
            (normed_all,) = exchange(10 + layer, [normed])
        normed_all = normed_all.reshape(row_count, width)
        query_rows = matmul_f32(normed, query_full).astype(bf16).astype(f32)
        key_rows = matmul_f32(normed_all, key_full).astype(bf16).astype(f32)
        values_all = matmul_f32(normed_all, value_full).astype(bf16)
        query_turned = rotate(query_rows.reshape(own_rows, HEADS, HEAD_DIM), cosine, sine)
        query_turned = query_turned.reshape(own_rows, -1).astype(bf16)
        keys_all = rotate(key_rows.reshape(row_count, KV_HEADS, HEAD_DIM), cos_all, sin_all)
        keys_all = keys_all.reshape(row_count, -1).astype(bf16)
        mixed, log_total = attend(query_turned, keys_all, values_all, allowed)
        mixed = mixed.astype(bf16)
        residual = residual + inner_cols(mixed, mix_turned)
        attend_saved.append(
            (
                rows_f32,
                row_scale,
                normed_all,
                query_turned,
                keys_all,
                values_all,
                log_total,
                mixed,
            )
        )
        rows_two, scale_two, normed_two = norm_in(residual, feed_gain[layer])
        (normed_two,) = exchange(20 + layer, [normed_two])
        normed_two = normed_two.reshape(row_count, width)
        gate_full, up_full, down_turned = feed_full[layer]
        gate_out = matmul_f32(normed_two, gate_full)
        up_out = matmul_f32(normed_two, up_full)
        hidden = (jax.nn.silu(gate_out) * up_out).astype(bf16)
        part = inner_cols(hidden, down_turned).astype(bf16).reshape(mp, own_rows, width)
        (part,) = exchange(30 + layer, (), (), [part])
        residual = residual + part
        feed_saved.append((rows_two, scale_two, normed_two, gate_out, up_out, hidden))
    block_output = residual.astype(bf16).reshape(own_rows // 2, 2 * width)

    grad_resid = cotangent.reshape(own_rows, width).astype(f32)
    attend_terms = [None] * LAYERS
    feed_terms = [None] * LAYERS
    grads = [None] * LAYERS
    feed_grads = [None] * LAYERS

    def attend_grads(layer, received):
        grad_all, mixed_cols, dqkv_cols = [a.reshape(row_count, -1) for a in received]
        normed_all = attend_saved[layer][2]
        return jnp.concatenate(
            [inner_rows(normed_all, dqkv_cols), inner_rows(grad_all, mixed_cols)], axis=1
        )

    late = None
    for layer in range(LAYERS - 1, -1, -1):
        rows_two, scale_two, normed_two, gate_out, up_out, hidden = feed_saved[layer]
        gate_full, up_full, down_turned = feed_full[layer]
        got = exchange(
            40 + layer,
            [grad_resid.astype(bf16)] + ([late[0]] if late else []),
            late[1:] if late else [],
        )
        grad_full = got[0].reshape(row_count, width)
        if late:
            grads[layer + 1] = attend_grads(layer + 1, got[1:])
        grad_hidden = matmul_f32(grad_full, down_turned)
        down_term = inner_rows(grad_full, hidden)
        sigmoid_gate = jax.nn.sigmoid(gate_out)
        grad_gate = (
            grad_hidden * up_out * sigmoid_gate * (1.0 + gate_out * (1.0 - sigmoid_gate))
        ).astype(bf16)
        grad_up = (grad_hidden * gate_out * sigmoid_gate).astype(bf16)
        grad_normed = (inner_cols(grad_gate, gate_full) + inner_cols(grad_up, up_full)).astype(bf16)
        (part,) = exchange(50 + layer, (), (), [grad_normed.reshape(mp, own_rows, width)])
        feed_grads[layer] = jnp.concatenate(
            [inner_rows(normed_two, grad_gate), inner_rows(normed_two, grad_up), down_term], axis=1
        )
        resid_grad, feed_terms[layer] = norm_back(
            part, rows_two, scale_two, feed_gain[layer]
        )
        grad_resid = grad_resid + resid_grad
        (
            rows_f32,
            row_scale,
            normed_all,
            query_turned,
            keys_all,
            values_all,
            log_total,
            mixed,
        ) = attend_saved[layer]
        query_full, key_full, value_full, mix_turned = attend_full[layer]
        grad_low = grad_resid.astype(bf16)
        grad_mixed = matmul_f32(grad_low, mix_turned).astype(bf16)
        grad_query, grad_keys, grad_values = attend_back(
            query_turned, keys_all, values_all, allowed, log_total, grad_mixed
        )
        key_value = jnp.concatenate([grad_keys, grad_values], axis=1).astype(bf16)
        (key_value,) = exchange(
            60 + layer, (), (), [key_value.reshape(mp, own_rows, 2 * mp * kw)]
        )
        query_back = rotate(grad_query.reshape(own_rows, HEADS, HEAD_DIM), cosine, -sine)
        query_back = query_back.reshape(own_rows, -1).astype(bf16)
        key_back = rotate(
            key_value[:, : mp * kw].reshape(own_rows, KV_HEADS, HEAD_DIM), cosine, -sine
        )
        key_back = key_back.reshape(own_rows, -1).astype(bf16)
        value_back = key_value[:, mp * kw :].astype(bf16)
        grad_normed = (
            inner_cols(query_back, query_full)
            + inner_cols(key_back, key_full)
            + inner_cols(value_back, value_full)
        )
        resid_grad, attend_terms[layer] = norm_back(
            grad_normed, rows_f32, row_scale, attend_gain[layer]
        )
        grad_resid = grad_resid + resid_grad
        dqkv = jnp.concatenate(
            [a.reshape(own_rows, mp, -1) for a in (query_back, key_back, value_back)], axis=2
        )
        late = (
            grad_low,
            jnp.moveaxis(mixed.reshape(own_rows, mp, qw), 1, 0),
            jnp.moveaxis(dqkv, 1, 0),
        )
    gains = jnp.concatenate([jnp.stack(attend_terms), jnp.stack(feed_terms)], axis=0)
    gains = jnp.concatenate([gains, jnp.zeros((16 - 2 * LAYERS, width), f32)], axis=0)
    got = exchange(2, [late[0], gains], late[1:])
    grads[0] = attend_grads(0, (got[0], got[2], got[3]))
    gains = summed(got[1])
    grad_pack = jnp.stack(
        [jnp.concatenate([grads[i], feed_grads[i]], axis=1).astype(bf16) for i in range(LAYERS)]
    )
    grad_pack = jnp.moveaxis(grad_pack.reshape(LAYERS, dp, depth, total_width), 1, 0)
    total, gains = sum_grads(3, grad_pack.reshape(dp, LAYERS * depth, total_width), gains)
    total = total.reshape(LAYERS, depth, total_width)
    input_grad = grad_resid.reshape(own_rows // 2, 2 * width)
    return (
        block_output,
        input_grad,
        gains[:LAYERS],
        total[:, :, :qw],
        total[:, :, qw : qw + kw],
        total[:, :, qw + kw : qw + 2 * kw],
        jnp.swapaxes(total[:, :, qw + 2 * kw : aw], 1, 2),
        gains[LAYERS : 2 * LAYERS],
        total[:, :, aw : aw + ff],
        total[:, :, aw + ff : aw + 2 * ff],
        jnp.swapaxes(total[:, :, aw + 2 * ff :], 1, 2),
    )


def solution(mesh):
    in_specs = (
        P(("dp", "mp"), None),
        P("dp", None),
        P(),
        P(None, "dp", "mp"),
        P(None, "dp", "mp"),
        P(None, "dp", "mp"),
        P(None, "mp", "dp"),
        P(),
        P(None, "dp", "mp"),
        P(None, "dp", "mp"),
        P(None, "mp", "dp"),
        P(("dp", "mp"), None),
    )
    out_specs = (
        P(("dp", "mp"), None),
        P(("dp", "mp"), None),
        P(),
        P(None, "dp", "mp"),
        P(None, "dp", "mp"),
        P(None, "dp", "mp"),
        P(None, "mp", "dp"),
        P(),
        P(None, "dp", "mp"),
        P(None, "dp", "mp"),
        P(None, "mp", "dp"),
    )
    return jax.shard_map(
        on_device, mesh=mesh, in_specs=in_specs, out_specs=out_specs, check_vma=False
    )
```
